32 devices in a mesh: wide: 8 (over z, y), narrow: 4 (over x, core).
Axes of the slice: x: 2, y: 2, z: 4, core: 2. Of those that a mesh axis runs over, the one named last changes fastest.
Arguments:
- hist_features: float32 [16, 131072], P(None, ('wide', 'narrow')), may hold values from -6 to 6
- hist_weights: float32 [8, 131072], P(None, ('wide', 'narrow')), may hold values from -6 to 6
- anal_features: float32 [16, 8192], P(None, 'narrow'), may hold values from -6 to 6
- anal_weights: float32 [8, 8192], P(None, 'narrow'), may hold values from -6 to 6
- lengthscale: float32 [16], replicated, may hold values from 1.2 to 3
- amplitude: float32 [8], replicated, may hold values from 4 to 16
Outputs:
- anal_out: float32 [8, 8192], P(None, 'narrow')
- hist_out: float32 [8, 131072], P(None, ('wide', 'narrow'))
The draws below stay inside these ranges and needn't reach their ends.
All inputs are finite; a program needn't handle non-finite values.
Results may differ from the reference program's by a relative error of at most 0.00029.
Values sent between devices are 32-bit elements; how exact they have to be, the bound alone decides.
No kernel may reach another device: no remote copies, remote signals or barrier semaphores. Data moves between devices by JAX's collectives and lax.ppermute only.
A program may use at most 64 MiB of HBM per device.

```python
import math
import jax
import jax.numpy as jnp
from jax import lax

NFEAT = 16
NRHS = 8
H_DEV = 4096
ANAL = 8192
HIST = 131072


def common_offset(key, spread):
    return jax.random.uniform(key, (NFEAT, 1), jnp.float32, -spread, spread)


def draw_hist_features(key, part):
    offset = common_offset(key, 1.0)
    key = jax.random.fold_in(key, 11)
    base = jnp.clip(jax.random.normal(key, (NFEAT, HIST), jnp.float32), -5.0, 5.0)
    return base + offset


def draw_anal_features(key, part):
    offset = common_offset(key, 1.0)
    key = jax.random.fold_in(key, 13)
    base = jnp.clip(jax.random.normal(key, (NFEAT, ANAL), jnp.float32), -5.0, 5.0)
    return base + offset


def steps_of(stream_key, extent, shards, low, top_value):
    gain, own = 1.0, jax.random.fold_in(stream_key, 6)
    for position, blocks in shards:
        heights = jnp.exp(jax.random.uniform(jax.random.fold_in(own, position), (blocks,), jnp.float32, low / len(shards), top_value / len(shards)))
        gain = gain * jnp.repeat(heights, extent[position] // blocks).reshape([-1 if axis == position else 1 for axis in range(len(extent))])
    return gain


def gaussian(key, dims, scale, limit, cuts=(), kind=jnp.bfloat16):
    factor_of = steps_of(key, dims, cuts, -0.22, 0.18) if cuts else 1.0
    entries = jax.random.normal(key, dims, jnp.float32) * scale * factor_of
    return jnp.minimum(jnp.maximum(entries, -limit), limit).astype(kind)


def setup_inputs(seed: int = 0) -> dict:
    key_of = jax.random.split(jax.random.key(seed), 7)
    hist_features = draw_hist_features(jax.random.fold_in(key_of[6], 71), 0)
    hist_weights = gaussian(key_of[1], (NRHS, HIST), 1.0, 6.0, ((1, 32),), jnp.float32)
    anal_features = draw_anal_features(jax.random.fold_in(key_of[6], 71), 0)
    anal_weights = gaussian(key_of[3], (NRHS, ANAL), 1.0, 6.0, ((1, 4),), jnp.float32)
    lengthscale = jnp.clip(jnp.exp(jax.random.uniform(key_of[4], (NFEAT,), jnp.float32, math.log(1.2), math.log(3.0))), 1.2, 3.0)
    amplitude = jnp.clip(jnp.exp(jax.random.uniform(key_of[5], (NRHS,), jnp.float32, math.log(4.0), math.log(16.0))), 4.0, 16.0)
    return {"hist_features": hist_features, "hist_weights": hist_weights, "anal_features": anal_features, "anal_weights": anal_weights, "lengthscale": lengthscale, "amplitude": amplitude}


def scaled_rows(features, lengthscale):
    scaled = features / lengthscale[:, None]
    return (scaled, lax.optimization_barrier(jnp.sum(scaled * scaled, axis=0)))

def kernel_tile(left, left_norms, right, right_norms):
    cross = jnp.einsum('fa,fh->ah', left, right, precision=lax.Precision.HIGHEST)
    return jnp.exp(-0.5 * (left_norms[:, None] + right_norms[None, :] - 2.0 * cross))

def reference(hist_features, hist_weights, anal_features, anal_weights, lengthscale, amplitude):
    anal_scaled, anal_norms = scaled_rows(anal_features, lengthscale)
    hist_scaled, hist_norms = scaled_rows(hist_features, lengthscale)
    count_blocks = HIST // H_DEV

    def step(forward, index):
        offset = index * H_DEV
        right = lax.dynamic_slice_in_dim(hist_scaled, offset, H_DEV, 1)
        right_norms = lax.dynamic_slice_in_dim(hist_norms, offset, H_DEV, 0)
        right_weights = lax.dynamic_slice_in_dim(hist_weights, offset, H_DEV, 1)
        tile = kernel_tile(anal_scaled, anal_norms, right, right_norms)
        forward = forward + jnp.dot(right_weights, tile.T, precision=lax.Precision.HIGHEST, preferred_element_type=jnp.float32)
        piece = jnp.dot(anal_weights, tile, precision=lax.Precision.HIGHEST, preferred_element_type=jnp.float32)
        return (forward, piece)
    forward, pieces = lax.scan(step, jnp.zeros((NRHS, ANAL), jnp.float32), jnp.arange(count_blocks, dtype=jnp.int32))
    transposed = jnp.moveaxis(pieces, 0, 1).reshape(NRHS, HIST)
    anal_out = forward * (amplitude[:, None] / math.sqrt(HIST))
    hist_out = transposed * (amplitude[:, None] / math.sqrt(ANAL))
    return (anal_out, hist_out)
```

```python
import functools
import math

import jax
import jax.numpy as jnp
from jax import lax
from jax.experimental import pallas as pl
from jax.experimental.pallas import tpu as pltpu
from jax.sharding import PartitionSpec as P

F32 = jnp.float32
BF16 = jnp.bfloat16
DEPTH = 128
ROWS = 256
COLS = 256
AHEAD = 2


def round_bf16(x):
    return x.astype(BF16).astype(F32)


def split3(x):
    first = round_bf16(x)
    rest = x - first
    second = round_bf16(rest)
    return first, second, round_bf16(rest - second)


def scale_features(features, lengthscale):
    return features / lengthscale * math.sqrt(math.log2(math.e))


def norm_rows(scaled, own_first):
    norms = jnp.sum(scaled * scaled, axis=0, keepdims=True) * -0.5
    parts = split3(norms)
    row = lax.broadcasted_iota(jnp.int32, (16, scaled.shape[1]), 0)
    base = 0 if own_first else 3
    out = jnp.where(row < 6, 1.0, 0.0).astype(F32)
    for k, part in enumerate(parts):
        out = jnp.where(row == base + k, part, out)
    return out


def stack_anal(scaled):
    p1, p2, p3 = split3(scaled)
    zero = jnp.zeros((16, scaled.shape[1]), F32)
    return [p1, p1, p2, p2, p1, p3, norm_rows(scaled, True), zero]


def stack_hist(scaled):
    p1, p2, p3 = split3(scaled)
    zero = jnp.zeros((16, scaled.shape[1]), F32)
    return [p1, p2, p1, p2, p3, p1, norm_rows(scaled, False), zero]


def hi_lo(x):
    hi = x.astype(BF16)
    return hi, (x - hi.astype(F32)).astype(BF16)


def dot(left, right):
    return jnp.dot(left, right, preferred_element_type=F32)


def dot_nt(left, right):
    dims = (((1,), (1,)), ((), ()))
    return lax.dot_general(left, right, dims, preferred_element_type=F32)


def column(row):
    size = row.shape[1]
    at = lax.broadcasted_iota(jnp.int32, (size, size), 0)
    to = lax.broadcasted_iota(jnp.int32, (size, size), 1)
    return jnp.sum(jnp.where(at == to, row, 0.0), axis=1, keepdims=True)


def prep_kernel(fwd_scale, trans_scale, *refs):
    sources, (bst_ref, w_ref, own_ref) = refs[:6], refs[6:9]
    held, sems = refs[9:15], refs[15]
    copies = [
        pltpu.make_async_copy(source, target, sems.at[k])
        for k, (source, target) in enumerate(zip(sources, held))
    ]
    for copy in copies:
        copy.start()
    for copy in copies:
        copy.wait()
    hf_ref, hw_ref, af_ref, aw_ref, ls_ref, amp_ref = held
    hist = hf_ref.shape[1]
    lengthscale = column(ls_ref[...])
    amplitude = column(amp_ref[...])
    own_ref[0:16, :] = scale_features(af_ref[...], lengthscale)
    own_ref[16:24, :] = aw_ref[...] * (amplitude * trans_scale)
    for start in range(0, hist, COLS):
        cols = slice(start, start + COLS)
        stack = stack_hist(scale_features(hf_ref[:, cols], lengthscale))
        for k, rows in enumerate(stack):
            bst_ref[k * 16 : (k + 1) * 16, cols] = rows.astype(BF16)
        weights = hw_ref[:, cols] * (amplitude * fwd_scale)
        hi = round_bf16(weights)
        w_ref[:, cols] = jnp.concatenate([hi, weights - hi], axis=0).astype(BF16)


def tile_kernel(offset, length, want_fwd, want_trans, has_total, counts, *refs):
    refs = list(refs)
    pieces = [refs.pop(0) for _ in counts]
    bst_ref, w_ref = refs.pop(0), refs.pop(0)
    total_ref = refs.pop(0) if has_total else None
    fwd_refs = [refs.pop(0) for _ in counts] if want_fwd else []
    trans_ref = refs.pop(0) if want_trans else None
    anal_ref, left_refs, u_ref, tile_refs, fwd_ref, acc_ref = (
        refs[0],
        refs[1:3],
        refs[3],
        refs[4:6],
        refs[6],
        refs[7],
    )
    hist = bst_ref.shape[1]
    half = hist // 2
    blocks = length // ROWS

    for k, piece in enumerate(pieces):
        size = length // len(pieces)
        anal_ref[:, k * size : (k + 1) * size] = piece[:, offset : offset + size]
    if want_trans:
        u_hi, u_lo = hi_lo(anal_ref[16:24, :])
        u_ref[...] = jnp.concatenate([u_hi.astype(F32), u_lo.astype(F32)], axis=0).astype(BF16)
        acc_ref[...] = jnp.zeros_like(acc_ref)

    def rows_of(block):
        return pl.ds(pl.multiple_of(block * ROWS, ROWS), ROWS)

    def prep(block, slot):
        stack = jnp.concatenate(stack_anal(anal_ref[0:16, rows_of(block)]), axis=0)
        left_refs[slot][...] = stack.T.astype(BF16)

    def produce(slot, part, start):
        at = part * half + start
        exponent = dot(left_refs[slot][...], bst_ref[:, at : at + COLS])
        hi, lo = hi_lo(jnp.exp2(exponent))
        tile_refs[part][0:ROWS, start : start + COLS] = hi
        tile_refs[part][ROWS : 2 * ROWS, start : start + COLS] = lo

    def consume(part, start, u, fwd):
        tile = tile_refs[part][:, start : start + COLS]
        at = part * half + start
        if want_trans:
            acc_ref[:, at : at + COLS] += dot(u, tile)
        if want_fwd:
            fwd += dot_nt(w_ref[:, at : at + COLS], tile)
        return fwd

    def vectors(block):
        u = u_ref[:, rows_of(block)]
        return jnp.concatenate([u, u], axis=1)

    starts = range(0, half, COLS)
    made = [(0, 1), (1, 0), (1, 1), (0, 0)]
    makes = [(slot, part, start) for slot, part in made for start in starts]
    uses = [(k, part, start) for k in range(2) for part in range(2) for start in starts]

    prep(0, 0)
    for start in starts:
        produce(0, 0, start)

    @pl.loop(0, blocks // 2)
    def _(pair):
        block = pair * 2
        prep(block + 1, 1)
        us = [vectors(block), vectors(block + 1)]
        fwds = [jnp.zeros((16, 2 * ROWS), F32)] * 2
        for n in range(len(makes) + AHEAD):
            if n == len(makes) // 2:
                prep(jnp.minimum(block + 2, blocks - 1), 0)
            if n < len(makes):
                produce(*makes[n])
            if n >= AHEAD:
                k, part, start = uses[n - AHEAD]
                fwds[k] = consume(part, start, us[k], fwds[k])
        if want_fwd:
            for k, fwd in enumerate(fwds):
                flat = fwd[:, 0:ROWS] + fwd[:, ROWS : 2 * ROWS]
                fwd_ref[:, rows_of(block + k)] = flat[0:8] + flat[8:16]

    for k, ref in enumerate(fwd_refs):
        size = length // len(pieces)
        ref[...] = fwd_ref[:, k * size : (k + 1) * size]
    if want_trans:
        total = acc_ref[0:8, :] + acc_ref[8:16, :]
        trans_ref[...] = total + total_ref[...] if has_total else total


VMEM = pl.BlockSpec(memory_space=pltpu.VMEM)
PARAMS = pltpu.CompilerParams(vmem_limit_bytes=40 * 1024 * 1024)


def prepare(fwd_scale, trans_scale, *args):
    hist = args[0].shape[1]
    count = args[2].shape[1]
    return pl.pallas_call(
        functools.partial(prep_kernel, fwd_scale, trans_scale),
        out_shape=(
            jax.ShapeDtypeStruct((DEPTH, hist), BF16),
            jax.ShapeDtypeStruct((16, hist), BF16),
            jax.ShapeDtypeStruct((24, count), F32),
        ),
        in_specs=[pl.BlockSpec(memory_space=pltpu.HBM)] * 6,
        out_specs=(VMEM,) * 3,
        scratch_shapes=[pltpu.VMEM(arg.shape, F32) for arg in args]
        + [pltpu.SemaphoreType.DMA((6,))],
        compiler_params=PARAMS,
        name="prepare",
    )(*[pltpu.with_memory_space_constraint(arg, pltpu.HBM) for arg in args])


def tile_call(pieces, offset, length, total, bst, w, want_fwd=True, want_trans=True):
    hist = bst.shape[1]
    rows = length * len(pieces)
    kernel = functools.partial(
        tile_kernel, offset, rows, want_fwd, want_trans, total is not None, [length] * len(pieces)
    )
    args = [*pieces, bst, w]
    if total is not None:
        args.append(total)
    outs = []
    if want_fwd:
        outs += [jax.ShapeDtypeStruct((8, length), F32)] * len(pieces)
    if want_trans:
        outs.append(jax.ShapeDtypeStruct((8, hist), F32))
    out = pl.pallas_call(
        kernel,
        out_shape=tuple(outs),
        in_specs=[VMEM] * len(args),
        out_specs=(VMEM,) * len(outs),
        scratch_shapes=[
            pltpu.VMEM((24, rows), F32),
            pltpu.VMEM((ROWS, DEPTH), BF16),
            pltpu.VMEM((ROWS, DEPTH), BF16),
            pltpu.VMEM((16, rows), BF16),
            pltpu.VMEM((2 * ROWS, hist // 2), BF16),
            pltpu.VMEM((2 * ROWS, hist // 2), BF16),
            pltpu.VMEM((8, rows), F32),
            pltpu.VMEM((16, hist), F32),
        ],
        compiler_params=PARAMS,
        cost_estimate=pl.CostEstimate(
            flops=(1 + 2 * want_fwd + 2 * want_trans) * 2 * 256 * rows * hist,
            bytes_accessed=4 * 24 * rows + 4 * DEPTH * hist,
            transcendentals=rows * hist,
        ),
        name="covariance_tiles",
    )(*args)
    fwd = list(out[: len(pieces)]) if want_fwd else []
    return fwd, out[-1] if want_trans else total


def exchange(x, axis, distance):
    size = lax.axis_size(axis)
    return lax.ppermute(x, axis, [(k, k ^ distance) for k in range(size)])


def on_device(hist_features, hist_weights, anal_features, anal_weights, lengthscale, amplitude):
    hist = hist_features.shape[1]
    count = anal_features.shape[1]
    narrow = lax.axis_size("narrow")
    wide = lax.axis_size("wide")
    fwd_scale = 1.0 / math.sqrt(hist * wide * narrow)
    trans_scale = 1.0 / math.sqrt(count * narrow)
    bst, w, own = prepare(
        fwd_scale,
        trans_scale,
        hist_features,
        hist_weights,
        anal_features,
        anal_weights,
        lengthscale[None, :],
        amplitude[None, :],
    )
    pieces = [exchange(own, "narrow", k) for k in range(1, narrow)]
    call = functools.partial(tile_call, bst=bst, w=w)
    first = count // 2
    fwd_a, total = call([own], 0, first, None)
    others, total = call(pieces, 0, count, total)
    received = [exchange(fwd, "narrow", k + 1) for k, fwd in enumerate(others)]
    fwd_b, hist_out = call([own], first, count - first, total)
    forward = jnp.concatenate(fwd_a + fwd_b, axis=1)
    for term in received:
        forward = forward + term
    distance = 1
    while distance < wide:
        forward = forward + exchange(forward, "wide", distance)
        distance *= 2
    return forward, hist_out


def solution(mesh):
    in_specs = (
        P(None, ("wide", "narrow")),
        P(None, ("wide", "narrow")),
        P(None, "narrow"),
        P(None, "narrow"),
        P(),
        P(),
    )
    out_specs = (P(None, "narrow"), P(None, ("wide", "narrow")))
    return jax.shard_map(
        on_device, mesh=mesh, in_specs=in_specs, out_specs=out_specs, check_vma=False
    )
```

```python
import functools
import math

import jax
import jax.numpy as jnp
from jax import lax
from jax.experimental import pallas as pl
from jax.experimental.pallas import tpu as pltpu
from jax.sharding import PartitionSpec as P

F32 = jnp.float32
BF16 = jnp.bfloat16
DEPTH = 128
ROWS = 256
COLS = 256
AHEAD = 2


def round_bf16(x):
    return x.astype(BF16).astype(F32)


def split3(x):
    first = round_bf16(x)
    rest = x - first
    second = round_bf16(rest)
    return first, second, round_bf16(rest - second)


def scale_features(features, lengthscale):
    return features / lengthscale


def norm_rows(scaled, own_first):
    norms = jnp.sum(scaled * scaled, axis=0, keepdims=True) * -0.5
    parts = split3(norms)
    row = lax.broadcasted_iota(jnp.int32, (16, scaled.shape[1]), 0)
    base = 0 if own_first else 3
    out = jnp.where(row < 6, 1.0, 0.0).astype(F32)
    for k, part in enumerate(parts):
        out = jnp.where(row == base + k, part, out)
    return out


def stack_anal(scaled):
    p1, p2, p3 = split3(scaled)
    zero = jnp.zeros((16, scaled.shape[1]), F32)
    return [p1, p1, p2, p2, p1, p3, norm_rows(scaled, True), zero]


def stack_hist(scaled):
    p1, p2, p3 = split3(scaled)
    zero = jnp.zeros((16, scaled.shape[1]), F32)
    return [p1, p2, p1, p2, p3, p1, norm_rows(scaled, False), zero]


def hi_lo(x):
    hi = x.astype(BF16)
    return hi, (x - hi.astype(F32)).astype(BF16)


def dot(left, right):
    return jnp.dot(left, right, preferred_element_type=F32)


def dot_nt(left, right):
    dims = (((1,), (1,)), ((), ()))
    return lax.dot_general(left, right, dims, preferred_element_type=F32)


def column(row):
    size = row.shape[1]
    at = lax.broadcasted_iota(jnp.int32, (size, size), 0)
    to = lax.broadcasted_iota(jnp.int32, (size, size), 1)
    return jnp.sum(jnp.where(at == to, row, 0.0), axis=1, keepdims=True)


def prep_kernel(fwd_scale, trans_scale, *refs):
    sources, (bst_ref, w_ref, own_ref) = refs[:6], refs[6:9]
    held, sems = refs[9:15], refs[15]
    copies = [
        pltpu.make_async_copy(source, target, sems.at[k])
        for k, (source, target) in enumerate(zip(sources, held))
    ]
    for copy in copies:
        copy.start()
    for copy in copies:
        copy.wait()
    hf_ref, hw_ref, af_ref, aw_ref, ls_ref, amp_ref = held
    hist = hf_ref.shape[1]
    lengthscale = column(ls_ref[...])
    amplitude = column(amp_ref[...])
    own_ref[0:16, :] = scale_features(af_ref[...], lengthscale)
    own_ref[16:24, :] = aw_ref[...] * (amplitude * trans_scale)
    for start in range(0, hist, COLS):
        cols = slice(start, start + COLS)
        stack = stack_hist(scale_features(hf_ref[:, cols], lengthscale))
        for k, rows in enumerate(stack):
            bst_ref[k * 16 : (k + 1) * 16, cols] = rows.astype(BF16)
        weights = hw_ref[:, cols] * (amplitude * fwd_scale)
        hi = round_bf16(weights)
        w_ref[:, cols] = jnp.concatenate([hi, weights - hi], axis=0).astype(BF16)


def tile_kernel(offset, length, want_fwd, want_trans, has_total, counts, *refs):
    refs = list(refs)
    pieces = [refs.pop(0) for _ in counts]
    bst_ref, w_ref = refs.pop(0), refs.pop(0)
    total_ref = refs.pop(0) if has_total else None
    fwd_refs = [refs.pop(0) for _ in counts] if want_fwd else []
    trans_ref = refs.pop(0) if want_trans else None
    anal_ref, left_refs, u_ref, tile_refs, fwd_ref, acc_ref = (
        refs[0],
        refs[1:3],
        refs[3],
        refs[4:6],
        refs[6],
        refs[7],
    )
    hist = bst_ref.shape[1]
    half = hist // 2
    blocks = length // ROWS

    for k, piece in enumerate(pieces):
        size = length // len(pieces)
        anal_ref[:, k * size : (k + 1) * size] = piece[:, offset : offset + size]
    if want_trans:
        u_hi, u_lo = hi_lo(anal_ref[16:24, :])
        u_ref[...] = jnp.concatenate([u_hi.astype(F32), u_lo.astype(F32)], axis=0).astype(BF16)
        acc_ref[...] = jnp.zeros_like(acc_ref)

    def rows_of(block):
        return pl.ds(pl.multiple_of(block * ROWS, ROWS), ROWS)

    def prep(block, slot):
        stack = jnp.concatenate(stack_anal(anal_ref[0:16, rows_of(block)]), axis=0)
        left_refs[slot][...] = stack.T.astype(BF16)

    def produce(slot, part, start):
        at = part * half + start
        exponent = dot(left_refs[slot][...], bst_ref[:, at : at + COLS])
        hi, lo = hi_lo(jnp.exp(exponent))
        tile_refs[part][0:ROWS, start : start + COLS] = hi
        tile_refs[part][ROWS : 2 * ROWS, start : start + COLS] = lo

    def consume(part, start, u, fwd):
        tile = tile_refs[part][:, start : start + COLS]
        at = part * half + start
        if want_trans:
            acc_ref[:, at : at + COLS] += dot(u, tile)
        if want_fwd:
            fwd += dot_nt(w_ref[:, at : at + COLS], tile)
        return fwd

    def vectors(block):
        u = u_ref[:, rows_of(block)]
        return jnp.concatenate([u, u], axis=1)

    starts = range(0, half, COLS)
    made = [(0, 1), (1, 0), (1, 1), (0, 0)]
    makes = [(slot, part, start) for slot, part in made for start in starts]
    uses = [(k, part, start) for k in range(2) for part in range(2) for start in starts]

    prep(0, 0)
    for start in starts:
        produce(0, 0, start)

    @pl.loop(0, blocks // 2)
    def _(pair):
        block = pair * 2
        prep(block + 1, 1)
        us = [vectors(block), vectors(block + 1)]
        fwds = [jnp.zeros((16, 2 * ROWS), F32)] * 2
        for n in range(len(makes) + AHEAD):
            if n == len(makes) // 2:
                prep(jnp.minimum(block + 2, blocks - 1), 0)
            if n < len(makes):
                produce(*makes[n])
            if n >= AHEAD:
                k, part, start = uses[n - AHEAD]
                fwds[k] = consume(part, start, us[k], fwds[k])
        if want_fwd:
            for k, fwd in enumerate(fwds):
                flat = fwd[:, 0:ROWS] + fwd[:, ROWS : 2 * ROWS]
                fwd_ref[:, rows_of(block + k)] = flat[0:8] + flat[8:16]

    for k, ref in enumerate(fwd_refs):
        size = length // len(pieces)
        ref[...] = fwd_ref[:, k * size : (k + 1) * size]
    if want_trans:
        total = acc_ref[0:8, :] + acc_ref[8:16, :]
        trans_ref[...] = total + total_ref[...] if has_total else total


VMEM = pl.BlockSpec(memory_space=pltpu.VMEM)
PARAMS = pltpu.CompilerParams(vmem_limit_bytes=40 * 1024 * 1024)


def prepare(fwd_scale, trans_scale, *args):
    hist = args[0].shape[1]
    count = args[2].shape[1]
    return pl.pallas_call(
        functools.partial(prep_kernel, fwd_scale, trans_scale),
        out_shape=(
            jax.ShapeDtypeStruct((DEPTH, hist), BF16),
            jax.ShapeDtypeStruct((16, hist), BF16),
            jax.ShapeDtypeStruct((24, count), F32),
        ),
        in_specs=[pl.BlockSpec(memory_space=pltpu.HBM)] * 6,
        out_specs=(VMEM,) * 3,
        scratch_shapes=[pltpu.VMEM(arg.shape, F32) for arg in args]
        + [pltpu.SemaphoreType.DMA((6,))],
        compiler_params=PARAMS,
        name="prepare",
    )(*[pltpu.with_memory_space_constraint(arg, pltpu.HBM) for arg in args])


def tile_call(pieces, offset, length, total, bst, w, want_fwd=True, want_trans=True):
    hist = bst.shape[1]
    rows = length * len(pieces)
    kernel = functools.partial(
        tile_kernel, offset, rows, want_fwd, want_trans, total is not None, [length] * len(pieces)
    )
    args = [*pieces, bst, w]
    if total is not None:
        args.append(total)
    outs = []
    if want_fwd:
        outs += [jax.ShapeDtypeStruct((8, length), F32)] * len(pieces)
    if want_trans:
        outs.append(jax.ShapeDtypeStruct((8, hist), F32))
    out = pl.pallas_call(
        kernel,
        out_shape=tuple(outs),
        in_specs=[VMEM] * len(args),
        out_specs=(VMEM,) * len(outs),
        scratch_shapes=[
            pltpu.VMEM((24, rows), F32),
            pltpu.VMEM((ROWS, DEPTH), BF16),
            pltpu.VMEM((ROWS, DEPTH), BF16),
            pltpu.VMEM((16, rows), BF16),
            pltpu.VMEM((2 * ROWS, hist // 2), BF16),
            pltpu.VMEM((2 * ROWS, hist // 2), BF16),
            pltpu.VMEM((8, rows), F32),
            pltpu.VMEM((16, hist), F32),
        ],
        compiler_params=PARAMS,
        cost_estimate=pl.CostEstimate(
            flops=(1 + 2 * want_fwd + 2 * want_trans) * 2 * 256 * rows * hist,
            bytes_accessed=4 * 24 * rows + 4 * DEPTH * hist,
            transcendentals=rows * hist,
        ),
        name="covariance_tiles",
    )(*args)
    fwd = list(out[: len(pieces)]) if want_fwd else []
    return fwd, out[-1] if want_trans else total


def exchange(x, axis, distance):
    size = lax.axis_size(axis)
    return lax.ppermute(x, axis, [(k, k ^ distance) for k in range(size)])


def on_device(hist_features, hist_weights, anal_features, anal_weights, lengthscale, amplitude):
    hist = hist_features.shape[1]
    count = anal_features.shape[1]
    narrow = lax.axis_size("narrow")
    wide = lax.axis_size("wide")
    fwd_scale = 1.0 / math.sqrt(hist * wide * narrow)
    trans_scale = 1.0 / math.sqrt(count * narrow)
    bst, w, own = prepare(
        fwd_scale,
        trans_scale,
        hist_features,
        hist_weights,
        anal_features,
        anal_weights,
        lengthscale[None, :],
        amplitude[None, :],
    )
    pieces = [exchange(own, "narrow", k) for k in range(1, narrow)]
    call = functools.partial(tile_call, bst=bst, w=w)
    first = count // 2
    fwd_a, total = call([own], 0, first, None)
    others, total = call(pieces, 0, count, total)
    received = [exchange(fwd, "narrow", k + 1) for k, fwd in enumerate(others)]
    fwd_b, hist_out = call([own], first, count - first, total)
    forward = jnp.concatenate(fwd_a + fwd_b, axis=1)
    for term in received:
        forward = forward + term
    distance = 1
    while distance < wide:
        steps = [k * distance for k in range(1, min(4, wide // distance))]
        arrived = [exchange(forward, "wide", step) for step in steps]
        for term in arrived:
            forward = forward + term
        distance *= 4
    return forward, hist_out


def solution(mesh):
    in_specs = (
        P(None, ("wide", "narrow")),
        P(None, ("wide", "narrow")),
        P(None, "narrow"),
        P(None, "narrow"),
        P(),
        P(),
    )
    out_specs = (P(None, "narrow"), P(None, ("wide", "narrow")))
    return jax.shard_map(
        on_device, mesh=mesh, in_specs=in_specs, out_specs=out_specs, check_vma=False
    )
```

```python
import functools
import math

import jax
import jax.numpy as jnp
from jax import lax
from jax.experimental import pallas as pl
from jax.experimental.pallas import tpu as pltpu
from jax.sharding import PartitionSpec as P

F32 = jnp.float32
BF16 = jnp.bfloat16
DEPTH = 128
ROWS = 256
COLS = 256
GROUP = 1024
AHEAD = 2


def round_bf16(x):
    return x.astype(BF16).astype(F32)


def split3(x):
    first = round_bf16(x)
    rest = x - first
    second = round_bf16(rest)
    return first, second, round_bf16(rest - second)


def scale_features(features, lengthscale):
    return features / lengthscale * math.sqrt(math.log2(math.e))


def norm_rows(scaled, own_first):
    norms = jnp.sum(scaled * scaled, axis=0, keepdims=True) * -0.5
    parts = split3(norms)
    row = lax.broadcasted_iota(jnp.int32, (16, scaled.shape[1]), 0)
    base = 0 if own_first else 3
    out = jnp.where(row < 6, 1.0, 0.0).astype(F32)
    for k, part in enumerate(parts):
        out = jnp.where(row == base + k, part, out)
    return out


def stack_anal(scaled):
    p1, p2, p3 = split3(scaled)
    zero = jnp.zeros((16, scaled.shape[1]), F32)
    return [p1, p1, p2, p2, p1, p3, norm_rows(scaled, True), zero]


def stack_hist(scaled):
    p1, p2, p3 = split3(scaled)
    zero = jnp.zeros((16, scaled.shape[1]), F32)
    return [p1, p2, p1, p2, p3, p1, norm_rows(scaled, False), zero]


def hi_lo(x):
    hi = x.astype(BF16)
    return hi, (x - hi.astype(F32)).astype(BF16)


def dot(left, right):
    return jnp.dot(left, right, preferred_element_type=F32)


def column(row):
    size = row.shape[1]
    at = lax.broadcasted_iota(jnp.int32, (size, size), 0)
    to = lax.broadcasted_iota(jnp.int32, (size, size), 1)
    return jnp.sum(jnp.where(at == to, row, 0.0), axis=1, keepdims=True)


def prep_kernel(fwd_scale, trans_scale, *refs):
    sources, (bst_ref, w_ref, own_ref) = refs[:6], refs[6:9]
    held, sems = refs[9:15], refs[15]
    copies = [
        pltpu.make_async_copy(source, target, sems.at[k])
        for k, (source, target) in enumerate(zip(sources, held))
    ]
    for copy in copies:
        copy.start()
    for copy in copies:
        copy.wait()
    hf_ref, hw_ref, af_ref, aw_ref, ls_ref, amp_ref = held
    hist = hf_ref.shape[1]
    lengthscale = column(ls_ref[...])
    amplitude = column(amp_ref[...])
    own_ref[0:16, :] = scale_features(af_ref[...], lengthscale)
    own_ref[16:24, :] = aw_ref[...] * (amplitude * trans_scale)
    for start in range(0, hist, COLS):
        cols = slice(start, start + COLS)
        stack = stack_hist(scale_features(hf_ref[:, cols], lengthscale))
        for k, rows in enumerate(stack):
            bst_ref[k * 16 : (k + 1) * 16, cols] = rows.astype(BF16)
        weights = hw_ref[:, cols] * (amplitude * fwd_scale)
        hi = round_bf16(weights)
        pad = jnp.zeros((DEPTH - 16, COLS), F32)
        w_ref[cols, :] = jnp.concatenate([hi, weights - hi, pad], axis=0).T.astype(BF16)


def tile_kernel(offset, length, want_fwd, want_trans, has_total, counts, *refs):
    refs = list(refs)
    pieces = [refs.pop(0) for _ in counts]
    bst_ref, w_ref = refs.pop(0), refs.pop(0)
    total_ref = refs.pop(0) if has_total else None
    fwd_refs = [refs.pop(0) for _ in counts] if want_fwd else []
    trans_ref = refs.pop(0) if want_trans else None
    anal_ref, left_refs, u_ref, tile_refs, fwd_ref, acc_ref = (
        refs[0],
        refs[1:3],
        refs[3],
        refs[4:6],
        refs[6],
        refs[7],
    )
    hist = bst_ref.shape[1]
    half = hist // 2
    group = min(GROUP, half)
    blocks = length // ROWS

    for k, piece in enumerate(pieces):
        size = length // len(pieces)
        anal_ref[:, k * size : (k + 1) * size] = piece[:, offset : offset + size]
    if want_trans:
        u_hi, u_lo = hi_lo(anal_ref[16:24, :])
        u_ref[...] = jnp.concatenate([u_hi.astype(F32), u_lo.astype(F32)], axis=0).astype(BF16)
        acc_ref[...] = jnp.zeros_like(acc_ref)

    def rows_of(block):
        return pl.ds(pl.multiple_of(block * ROWS, ROWS), ROWS)

    def prep(block, slot):
        stack = jnp.concatenate(stack_anal(anal_ref[0:16, rows_of(block)]), axis=0)
        left_refs[slot][...] = stack.T.astype(BF16)

    def produce(slot, part, start):
        at = part * half + start
        exponent = dot(left_refs[slot][...], bst_ref[:, at : at + COLS])
        hi, lo = hi_lo(jnp.exp2(exponent))
        tile_refs[part][0:ROWS, start : start + COLS] = hi
        tile_refs[part][ROWS : 2 * ROWS, start : start + COLS] = lo

    def consume(part, start, u, sums):
        at = part * half + start
        if want_trans:
            acc_ref[:, at : at + COLS] += dot(u, tile_refs[part][:, start : start + COLS])
        if want_fwd:
            first, step = start // group * group, start % group // COLS
            share = 2 * ROWS * COLS // group
            rows = slice(step * share, (step + 1) * share)
            left = tile_refs[part][rows, first : first + group]
            value = dot(left, w_ref[part * half + first : part * half + first + group, :])
            sums[step] = value if sums[step] is None else sums[step] + value

    def vectors(block):
        u = u_ref[:, rows_of(block)]
        return jnp.concatenate([u, u], axis=1)

    starts = range(0, half, COLS)
    made = [(0, 1), (1, 0), (1, 1), (0, 0)]
    makes = [(slot, part, start) for slot, part in made for start in starts]
    uses = [(k, part, start) for k in range(2) for part in range(2) for start in starts]

    prep(0, 0)
    for start in starts:
        produce(0, 0, start)

    @pl.loop(0, blocks // 2)
    def _(pair):
        block = pair * 2
        prep(block + 1, 1)
        us = [vectors(block), vectors(block + 1)]
        fwds = [[None] * (group // COLS) for _ in us]
        for n in range(len(makes) + AHEAD):
            if n == len(makes) // 2:
                prep(jnp.minimum(block + 2, blocks - 1), 0)
            if n < len(makes):
                produce(*makes[n])
            if n >= AHEAD:
                k, part, start = uses[n - AHEAD]
                consume(part, start, us[k], fwds[k])
        if want_fwd:
            for k, sums in enumerate(fwds):
                fwd = jnp.concatenate(sums, axis=0)
                flat = (fwd[0:ROWS] + fwd[ROWS : 2 * ROWS]).T
                fwd_ref[:, rows_of(block + k)] = flat[0:8] + flat[8:16]

    for k, ref in enumerate(fwd_refs):
        size = length // len(pieces)
        ref[...] = fwd_ref[:, k * size : (k + 1) * size]
    if want_trans:
        total = acc_ref[0:8, :] + acc_ref[8:16, :]
        trans_ref[...] = total + total_ref[...] if has_total else total


VMEM = pl.BlockSpec(memory_space=pltpu.VMEM)
PARAMS = pltpu.CompilerParams(vmem_limit_bytes=40 * 1024 * 1024)


def prepare(fwd_scale, trans_scale, *args):
    hist = args[0].shape[1]
    count = args[2].shape[1]
    return pl.pallas_call(
        functools.partial(prep_kernel, fwd_scale, trans_scale),
        out_shape=(
            jax.ShapeDtypeStruct((DEPTH, hist), BF16),
            jax.ShapeDtypeStruct((hist, DEPTH), BF16),
            jax.ShapeDtypeStruct((24, count), F32),
        ),
        in_specs=[pl.BlockSpec(memory_space=pltpu.HBM)] * 6,
        out_specs=(VMEM,) * 3,
        scratch_shapes=[pltpu.VMEM(arg.shape, F32) for arg in args]
        + [pltpu.SemaphoreType.DMA((6,))],
        compiler_params=PARAMS,
        name="prepare",
    )(*[pltpu.with_memory_space_constraint(arg, pltpu.HBM) for arg in args])


def tile_call(pieces, offset, length, total, bst, w, want_fwd=True, want_trans=True):
    hist = bst.shape[1]
    rows = length * len(pieces)
    kernel = functools.partial(
        tile_kernel, offset, rows, want_fwd, want_trans, total is not None, [length] * len(pieces)
    )
    args = [*pieces, bst, w]
    if total is not None:
        args.append(total)
    outs = []
    if want_fwd:
        outs += [jax.ShapeDtypeStruct((8, length), F32)] * len(pieces)
    if want_trans:
        outs.append(jax.ShapeDtypeStruct((8, hist), F32))
    out = pl.pallas_call(
        kernel,
        out_shape=tuple(outs),
        in_specs=[VMEM] * len(args),
        out_specs=(VMEM,) * len(outs),
        scratch_shapes=[
            pltpu.VMEM((24, rows), F32),
            pltpu.VMEM((ROWS, DEPTH), BF16),
            pltpu.VMEM((ROWS, DEPTH), BF16),
            pltpu.VMEM((16, rows), BF16),
            pltpu.VMEM((2 * ROWS, hist // 2), BF16),
            pltpu.VMEM((2 * ROWS, hist // 2), BF16),
            pltpu.VMEM((8, rows), F32),
            pltpu.VMEM((16, hist), F32),
        ],
        compiler_params=PARAMS,
        cost_estimate=pl.CostEstimate(
            flops=(1 + 2 * want_fwd + 2 * want_trans) * 2 * 256 * rows * hist,
            bytes_accessed=4 * 24 * rows + 4 * DEPTH * hist,
            transcendentals=rows * hist,
        ),
        name="covariance_tiles",
    )(*args)
    fwd = list(out[: len(pieces)]) if want_fwd else []
    return fwd, out[-1] if want_trans else total


def exchange(x, axis, distance):
    size = lax.axis_size(axis)
    return lax.ppermute(x, axis, [(k, k ^ distance) for k in range(size)])


def on_device(hist_features, hist_weights, anal_features, anal_weights, lengthscale, amplitude):
    hist = hist_features.shape[1]
    count = anal_features.shape[1]
    narrow = lax.axis_size("narrow")
    wide = lax.axis_size("wide")
    fwd_scale = 1.0 / math.sqrt(hist * wide * narrow)
    trans_scale = 1.0 / math.sqrt(count * narrow)
    bst, w, own = prepare(
        fwd_scale,
        trans_scale,
        hist_features,
        hist_weights,
        anal_features,
        anal_weights,
        lengthscale[None, :],
        amplitude[None, :],
    )
    pieces = [exchange(own, "narrow", k) for k in range(1, narrow)]
    call = functools.partial(tile_call, bst=bst, w=w)
    first = count // 2
    fwd_a, total = call([own], 0, first, None)
    others, total = call(pieces, 0, count, total)
    received = [exchange(fwd, "narrow", k + 1) for k, fwd in enumerate(others)]
    fwd_b, hist_out = call([own], first, count - first, total)
    forward = jnp.concatenate(fwd_a + fwd_b, axis=1)
    for term in received:
        forward = forward + term
    distance = 1
    while distance < wide:
        steps = [k * distance for k in range(1, min(4, wide // distance))]
        arrived = [exchange(forward, "wide", step) for step in steps]
        for term in arrived:
            forward = forward + term
        distance *= 4
    return forward, hist_out


def solution(mesh):
    in_specs = (
        P(None, ("wide", "narrow")),
        P(None, ("wide", "narrow")),
        P(None, "narrow"),
        P(None, "narrow"),
        P(),
        P(),
    )
    out_specs = (P(None, "narrow"), P(None, ("wide", "narrow")))
    return jax.shard_map(
        on_device, mesh=mesh, in_specs=in_specs, out_specs=out_specs, check_vma=False
    )
```

```python
import functools
import math

import jax
import jax.numpy as jnp
from jax import lax
from jax.experimental import pallas as pl
from jax.experimental.pallas import tpu as pltpu
from jax.sharding import PartitionSpec as P

F32 = jnp.float32
BF16 = jnp.bfloat16
DEPTH = 128
ROWS = 256
COLS = 256
GROUP = 512
AHEAD = 2


def round_bf16(x):
    return x.astype(BF16).astype(F32)


def split3(x):
    first = round_bf16(x)
    rest = x - first
    second = round_bf16(rest)
    return first, second, round_bf16(rest - second)


def scale_features(features, lengthscale):
    return features / lengthscale * math.sqrt(math.log2(math.e))


def norm_rows(scaled, own_first):
    norms = jnp.sum(scaled * scaled, axis=0, keepdims=True) * -0.5
    parts = split3(norms)
    row = lax.broadcasted_iota(jnp.int32, (16, scaled.shape[1]), 0)
    base = 0 if own_first else 3
    out = jnp.where(row < 6, 1.0, 0.0).astype(F32)
    for k, part in enumerate(parts):
        out = jnp.where(row == base + k, part, out)
    return out


def stack_anal(scaled):
    p1, p2, p3 = split3(scaled)
    zero = jnp.zeros((16, scaled.shape[1]), F32)
    return [p1, p1, p2, p2, p1, p3, norm_rows(scaled, True), zero]


def stack_hist(scaled):
    p1, p2, p3 = split3(scaled)
    zero = jnp.zeros((16, scaled.shape[1]), F32)
    return [p1, p2, p1, p2, p3, p1, norm_rows(scaled, False), zero]


def hi_lo(x):
    hi = x.astype(BF16)
    return hi, (x - hi.astype(F32)).astype(BF16)


def dot(left, right):
    return jnp.dot(left, right, preferred_element_type=F32)


def dot_nt(left, right):
    dims = (((1,), (1,)), ((), ()))
    return lax.dot_general(left, right, dims, preferred_element_type=F32)


def column(row):
    size = row.shape[1]
    at = lax.broadcasted_iota(jnp.int32, (size, size), 0)
    to = lax.broadcasted_iota(jnp.int32, (size, size), 1)
    return jnp.sum(jnp.where(at == to, row, 0.0), axis=1, keepdims=True)


def prep_kernel(fwd_scale, trans_scale, *refs):
    sources, (bst_ref, w_ref, wt_ref, own_ref) = refs[:6], refs[6:10]
    held, sems = refs[10:16], refs[16]
    copies = [
        pltpu.make_async_copy(source, target, sems.at[k])
        for k, (source, target) in enumerate(zip(sources, held))
    ]
    for copy in copies:
        copy.start()
    for copy in copies:
        copy.wait()
    hf_ref, hw_ref, af_ref, aw_ref, ls_ref, amp_ref = held
    hist = hf_ref.shape[1]
    lengthscale = column(ls_ref[...])
    amplitude = column(amp_ref[...])
    own_ref[0:16, :] = scale_features(af_ref[...], lengthscale)
    own_ref[16:24, :] = aw_ref[...] * (amplitude * trans_scale)
    for start in range(0, hist, COLS):
        cols = slice(start, start + COLS)
        stack = stack_hist(scale_features(hf_ref[:, cols], lengthscale))
        for k, rows in enumerate(stack):
            bst_ref[k * 16 : (k + 1) * 16, cols] = rows.astype(BF16)
        weights = hw_ref[:, cols] * (amplitude * fwd_scale)
        hi = round_bf16(weights)
        pad = jnp.zeros((DEPTH - 16, COLS), F32)
        w_ref[:, cols] = jnp.concatenate([hi, weights - hi], axis=0).astype(BF16)
        wt_ref[cols, :] = jnp.concatenate([hi, weights - hi, pad], axis=0).T.astype(BF16)


def tile_kernel(offset, length, want_fwd, want_trans, has_total, counts, *refs):
    refs = list(refs)
    pieces = [refs.pop(0) for _ in counts]
    bst_ref, w_ref, wt_ref = refs.pop(0), refs.pop(0), refs.pop(0)
    total_ref = refs.pop(0) if has_total else None
    fwd_refs = [refs.pop(0) for _ in counts] if want_fwd else []
    trans_ref = refs.pop(0) if want_trans else None
    anal_ref, left_refs, u_ref, tile_refs, fwd_ref, acc_ref = (
        refs[0],
        refs[1:3],
        refs[3],
        refs[4:6],
        refs[6],
        refs[7],
    )
    hist = bst_ref.shape[1]
    half = hist // 2
    group = min(GROUP, half)
    blocks = length // ROWS

    for k, piece in enumerate(pieces):
        size = length // len(pieces)
        anal_ref[:, k * size : (k + 1) * size] = piece[:, offset : offset + size]
    if want_trans:
        u_hi, u_lo = hi_lo(anal_ref[16:24, :])
        u_ref[...] = jnp.concatenate([u_hi.astype(F32), u_lo.astype(F32)], axis=0).astype(BF16)
        acc_ref[...] = jnp.zeros_like(acc_ref)

    def rows_of(block):
        return pl.ds(pl.multiple_of(block * ROWS, ROWS), ROWS)

    def prep(block, slot):
        stack = jnp.concatenate(stack_anal(anal_ref[0:16, rows_of(block)]), axis=0)
        left_refs[slot][...] = stack.T.astype(BF16)

    def produce(slot, part, start):
        at = part * half + start
        exponent = dot(left_refs[slot][...], bst_ref[:, at : at + COLS])
        hi, lo = hi_lo(jnp.exp2(exponent))
        tile_refs[part][0:ROWS, start : start + COLS] = hi
        tile_refs[part][ROWS : 2 * ROWS, start : start + COLS] = lo

    def consume(part, start, u, sums):
        at = part * half + start
        if want_trans:
            acc_ref[:, at : at + COLS] += dot(u, tile_refs[part][:, start : start + COLS])
        if want_fwd:
            first, step = start // group * group, start % group // COLS
            share = ROWS * COLS // group
            left = tile_refs[part][step * share : (step + 1) * share, first : first + group]
            value = dot(left, wt_ref[part * half + first : part * half + first + group, :])
            sums[step] = value if sums[step] is None else sums[step] + value
            low = tile_refs[part][ROWS : 2 * ROWS, start : start + COLS]
            value = dot_nt(w_ref[:, at : at + COLS], low)
            sums[-1] = value if sums[-1] is None else sums[-1] + value

    def vectors(block):
        u = u_ref[:, rows_of(block)]
        return jnp.concatenate([u, u], axis=1)

    starts = range(0, half, COLS)
    made = [(0, 1), (1, 0), (1, 1), (0, 0)]
    makes = [(slot, part, start) for slot, part in made for start in starts]
    uses = [(k, part, start) for k in range(2) for part in range(2) for start in starts]

    prep(0, 0)
    for start in starts:
        produce(0, 0, start)

    @pl.loop(0, blocks // 2)
    def _(pair):
        block = pair * 2
        prep(block + 1, 1)
        us = [vectors(block), vectors(block + 1)]
        fwds = [[None] * (group // COLS + 1) for _ in us]
        for n in range(len(makes) + AHEAD):
            if n == len(makes) // 2:
                prep(jnp.minimum(block + 2, blocks - 1), 0)
            if n < len(makes):
                produce(*makes[n])
            if n >= AHEAD:
                k, part, start = uses[n - AHEAD]
                consume(part, start, us[k], fwds[k])
        if want_fwd:
            for k, sums in enumerate(fwds):
                flat = jnp.concatenate(sums[:-1], axis=0).T[0:16] + sums[-1]
                fwd_ref[:, rows_of(block + k)] = flat[0:8] + flat[8:16]

    for k, ref in enumerate(fwd_refs):
        size = length // len(pieces)
        ref[...] = fwd_ref[:, k * size : (k + 1) * size]
    if want_trans:
        total = acc_ref[0:8, :] + acc_ref[8:16, :]
        trans_ref[...] = total + total_ref[...] if has_total else total


VMEM = pl.BlockSpec(memory_space=pltpu.VMEM)
PARAMS = pltpu.CompilerParams(vmem_limit_bytes=40 * 1024 * 1024)


def prepare(fwd_scale, trans_scale, *args):
    hist = args[0].shape[1]
    count = args[2].shape[1]
    return pl.pallas_call(
        functools.partial(prep_kernel, fwd_scale, trans_scale),
        out_shape=(
            jax.ShapeDtypeStruct((DEPTH, hist), BF16),
            jax.ShapeDtypeStruct((16, hist), BF16),
            jax.ShapeDtypeStruct((hist, DEPTH), BF16),
            jax.ShapeDtypeStruct((24, count), F32),
        ),
        in_specs=[pl.BlockSpec(memory_space=pltpu.HBM)] * 6,
        out_specs=(VMEM,) * 4,
        scratch_shapes=[pltpu.VMEM(arg.shape, F32) for arg in args]
        + [pltpu.SemaphoreType.DMA((6,))],
        compiler_params=PARAMS,
        name="prepare",
    )(*[pltpu.with_memory_space_constraint(arg, pltpu.HBM) for arg in args])


def tile_call(pieces, offset, length, total, bst, w, wt, want_fwd=True, want_trans=True):
    hist = bst.shape[1]
    rows = length * len(pieces)
    kernel = functools.partial(
        tile_kernel, offset, rows, want_fwd, want_trans, total is not None, [length] * len(pieces)
    )
    args = [*pieces, bst, w, wt]
    if total is not None:
        args.append(total)
    outs = []
    if want_fwd:
        outs += [jax.ShapeDtypeStruct((8, length), F32)] * len(pieces)
    if want_trans:
        outs.append(jax.ShapeDtypeStruct((8, hist), F32))
    out = pl.pallas_call(
        kernel,
        out_shape=tuple(outs),
        in_specs=[VMEM] * len(args),
        out_specs=(VMEM,) * len(outs),
        scratch_shapes=[
            pltpu.VMEM((24, rows), F32),
            pltpu.VMEM((ROWS, DEPTH), BF16),
            pltpu.VMEM((ROWS, DEPTH), BF16),
            pltpu.VMEM((16, rows), BF16),
            pltpu.VMEM((2 * ROWS, hist // 2), BF16),
            pltpu.VMEM((2 * ROWS, hist // 2), BF16),
            pltpu.VMEM((8, rows), F32),
            pltpu.VMEM((16, hist), F32),
        ],
        compiler_params=PARAMS,
        cost_estimate=pl.CostEstimate(
            flops=(1 + 2 * want_fwd + 2 * want_trans) * 2 * 256 * rows * hist,
            bytes_accessed=4 * 24 * rows + 4 * DEPTH * hist,
            transcendentals=rows * hist,
        ),
        name="covariance_tiles",
    )(*args)
    fwd = list(out[: len(pieces)]) if want_fwd else []
    return fwd, out[-1] if want_trans else total


def exchange(x, axis, distance):
    size = lax.axis_size(axis)
    return lax.ppermute(x, axis, [(k, k ^ distance) for k in range(size)])


def on_device(hist_features, hist_weights, anal_features, anal_weights, lengthscale, amplitude):
    hist = hist_features.shape[1]
    count = anal_features.shape[1]
    narrow = lax.axis_size("narrow")
    wide = lax.axis_size("wide")
    fwd_scale = 1.0 / math.sqrt(hist * wide * narrow)
    trans_scale = 1.0 / math.sqrt(count * narrow)
    bst, w, wt, own = prepare(
        fwd_scale,
        trans_scale,
        hist_features,
        hist_weights,
        anal_features,
        anal_weights,
        lengthscale[None, :],
        amplitude[None, :],
    )
    pieces = [exchange(own, "narrow", k) for k in range(1, narrow)]
    call = functools.partial(tile_call, bst=bst, w=w, wt=wt)
    first = count // 2
    fwd_a, total = call([own], 0, first, None)
    others, total = call(pieces, 0, count, total)
    received = [exchange(fwd, "narrow", k + 1) for k, fwd in enumerate(others)]
    fwd_b, hist_out = call([own], first, count - first, total)
    forward = jnp.concatenate(fwd_a + fwd_b, axis=1)
    for term in received:
        forward = forward + term
    distance = 1
    while distance < wide:
        steps = [k * distance for k in range(1, min(4, wide // distance))]
        arrived = [exchange(forward, "wide", step) for step in steps]
        for term in arrived:
            forward = forward + term
        distance *= 4
    return forward, hist_out


def solution(mesh):
    in_specs = (
        P(None, ("wide", "narrow")),
        P(None, ("wide", "narrow")),
        P(None, "narrow"),
        P(None, "narrow"),
        P(),
        P(),
    )
    out_specs = (P(None, "narrow"), P(None, ("wide", "narrow")))
    return jax.shard_map(
        on_device, mesh=mesh, in_specs=in_specs, out_specs=out_specs, check_vma=False
    )
```

```python
import functools
import math

import jax
import jax.numpy as jnp
from jax import lax
from jax.experimental import pallas as pl
from jax.experimental.pallas import tpu as pltpu
from jax.sharding import PartitionSpec as P

F32 = jnp.float32
BF16 = jnp.bfloat16
DEPTH = 128
ROWS = 256
COLS = 256
FLIP_ROUND = 2
FLIP_HI = 2
AHEAD = 2


def round_bf16(x):
    return x.astype(BF16).astype(F32)


def split3(x):
    first = round_bf16(x)
    rest = x - first
    second = round_bf16(rest)
    return first, second, round_bf16(rest - second)


def scale_features(features, lengthscale):
    return features / lengthscale * math.sqrt(math.log2(math.e))


def norm_rows(scaled, own_first):
    norms = jnp.sum(scaled * scaled, axis=0, keepdims=True) * -0.5
    parts = split3(norms)
    row = lax.broadcasted_iota(jnp.int32, (16, scaled.shape[1]), 0)
    base = 0 if own_first else 3
    out = jnp.where(row < 6, 1.0, 0.0).astype(F32)
    for k, part in enumerate(parts):
        out = jnp.where(row == base + k, part, out)
    return out


def stack_anal(scaled):
    p1, p2, p3 = split3(scaled)
    zero = jnp.zeros((16, scaled.shape[1]), F32)
    return [p1, p1, p2, p2, p1, p3, norm_rows(scaled, True), zero]


def stack_hist(scaled):
    p1, p2, p3 = split3(scaled)
    zero = jnp.zeros((16, scaled.shape[1]), F32)
    return [p1, p2, p1, p2, p3, p1, norm_rows(scaled, False), zero]


def hi_lo(x):
    hi = x.astype(BF16)
    return hi, (x - hi.astype(F32)).astype(BF16)


def dot(left, right):
    return jnp.dot(left, right, preferred_element_type=F32)


def dot_nt(left, right):
    dims = (((1,), (1,)), ((), ()))
    return lax.dot_general(left, right, dims, preferred_element_type=F32)


def column(row):
    size = row.shape[1]
    at = lax.broadcasted_iota(jnp.int32, (size, size), 0)
    to = lax.broadcasted_iota(jnp.int32, (size, size), 1)
    return jnp.sum(jnp.where(at == to, row, 0.0), axis=1, keepdims=True)


def prep_kernel(fwd_scale, trans_scale, *refs):
    sources, (bst_ref, w_ref, own_ref) = refs[:6], refs[6:9]
    held, sems = refs[9:15], refs[15]
    copies = [
        pltpu.make_async_copy(source, target, sems.at[k])
        for k, (source, target) in enumerate(zip(sources, held))
    ]
    for copy in copies:
        copy.start()
    for copy in copies:
        copy.wait()
    hf_ref, hw_ref, af_ref, aw_ref, ls_ref, amp_ref = held
    hist = hf_ref.shape[1]
    lengthscale = column(ls_ref[...])
    amplitude = column(amp_ref[...])
    own_ref[0:16, :] = scale_features(af_ref[...], lengthscale)
    own_ref[16:24, :] = aw_ref[...] * (amplitude * trans_scale)
    for start in range(0, hist, COLS):
        cols = slice(start, start + COLS)
        stack = stack_hist(scale_features(hf_ref[:, cols], lengthscale))
        for k, rows in enumerate(stack):
            bst_ref[k * 16 : (k + 1) * 16, cols] = rows.astype(BF16)
        weights = hw_ref[:, cols] * (amplitude * fwd_scale)
        hi = round_bf16(weights)
        w_ref[:, cols] = jnp.concatenate([hi, weights - hi], axis=0).astype(BF16)


def tile_kernel(offset, length, want_fwd, want_trans, has_total, counts, *refs):
    refs = list(refs)
    pieces = [refs.pop(0) for _ in counts]
    bst_ref, w_ref = refs.pop(0), refs.pop(0)
    total_ref = refs.pop(0) if has_total else None
    fwd_refs = [refs.pop(0) for _ in counts] if want_fwd else []
    trans_ref = refs.pop(0) if want_trans else None
    anal_ref, u_ref, fwd_ref, acc_ref = refs[0:4]
    left_refs, tile_refs, flip_refs = refs[4:6], refs[6:8], refs[8:10]
    hist = bst_ref.shape[1]
    half = hist // 2
    blocks = length // ROWS

    for k, piece in enumerate(pieces):
        size = length // len(pieces)
        anal_ref[:, k * size : (k + 1) * size] = piece[:, offset : offset + size]
    if want_trans:
        u_hi, u_lo = hi_lo(anal_ref[16:24, :])
        u_ref[...] = jnp.concatenate([u_hi.astype(F32), u_lo.astype(F32)], axis=0).astype(BF16)
        acc_ref[...] = jnp.zeros_like(acc_ref)

    def rows_of(block):
        return pl.ds(pl.multiple_of(block * ROWS, ROWS), ROWS)

    def prep(block, slot):
        stack = jnp.concatenate(stack_anal(anal_ref[0:16, rows_of(block)]), axis=0)
        left_refs[slot][...] = stack.T.astype(BF16)

    def flips_hi(start):
        return start // COLS % FLIP_ROUND < FLIP_HI

    def produce(slot, part, start):
        at = part * half + start
        exponent = dot(left_refs[slot][...], bst_ref[:, at : at + COLS])
        hi, lo = hi_lo(jnp.exp2(exponent))
        tile_refs[part][0:ROWS, start : start + COLS] = hi
        tile_refs[part][ROWS : 2 * ROWS, start : start + COLS] = lo
        if want_fwd:
            flip_refs[part][start : start + COLS, ROWS : 2 * ROWS] = lo.T
            if flips_hi(start):
                flip_refs[part][start : start + COLS, 0:ROWS] = hi.T

    def consume(part, start, u, fwd):
        tile = tile_refs[part][:, start : start + COLS]
        at = part * half + start
        if want_trans:
            acc_ref[:, at : at + COLS] += dot(u, tile)
        if want_fwd:
            w = w_ref[:, at : at + COLS]
            flip = flip_refs[part][start : start + COLS, :]
            if flips_hi(start):
                both = dot(w, flip)
                fwd += both[:, 0:ROWS] + both[:, ROWS : 2 * ROWS]
            else:
                fwd += dot_nt(w, tile[0:ROWS]) + dot(w, flip[:, ROWS : 2 * ROWS])
        return fwd

    def vectors(block):
        u = u_ref[:, rows_of(block)]
        return jnp.concatenate([u, u], axis=1)

    starts = range(0, half, COLS)
    made = [(0, 1), (1, 0), (1, 1), (0, 0)]
    makes = [(slot, part, start) for slot, part in made for start in starts]
    uses = [(k, part, start) for k in range(2) for part in range(2) for start in starts]

    prep(0, 0)
    for start in starts:
        produce(0, 0, start)

    @pl.loop(0, blocks // 2)
    def _(pair):
        block = pair * 2
        prep(block + 1, 1)
        us = [vectors(block), vectors(block + 1)]
        fwds = [jnp.zeros((16, ROWS), F32)] * 2
        for n in range(len(makes) + AHEAD):
            if n == len(makes) // 2:
                prep(jnp.minimum(block + 2, blocks - 1), 0)
            if n < len(makes):
                produce(*makes[n])
            if n >= AHEAD:
                k, part, start = uses[n - AHEAD]
                fwds[k] = consume(part, start, us[k], fwds[k])
        if want_fwd:
            for k, fwd in enumerate(fwds):
                fwd_ref[:, rows_of(block + k)] = fwd[0:8] + fwd[8:16]

    for k, ref in enumerate(fwd_refs):
        size = length // len(pieces)
        ref[...] = fwd_ref[:, k * size : (k + 1) * size]
    if want_trans:
        total = acc_ref[0:8, :] + acc_ref[8:16, :]
        trans_ref[...] = total + total_ref[...] if has_total else total


VMEM = pl.BlockSpec(memory_space=pltpu.VMEM)
PARAMS = pltpu.CompilerParams(vmem_limit_bytes=40 * 1024 * 1024)


def prepare(fwd_scale, trans_scale, *args):
    hist = args[0].shape[1]
    count = args[2].shape[1]
    return pl.pallas_call(
        functools.partial(prep_kernel, fwd_scale, trans_scale),
        out_shape=(
            jax.ShapeDtypeStruct((DEPTH, hist), BF16),
            jax.ShapeDtypeStruct((16, hist), BF16),
            jax.ShapeDtypeStruct((24, count), F32),
        ),
        in_specs=[pl.BlockSpec(memory_space=pltpu.HBM)] * 6,
        out_specs=(VMEM,) * 3,
        scratch_shapes=[pltpu.VMEM(arg.shape, F32) for arg in args]
        + [pltpu.SemaphoreType.DMA((6,))],
        compiler_params=PARAMS,
        name="prepare",
    )(*[pltpu.with_memory_space_constraint(arg, pltpu.HBM) for arg in args])


def tile_call(pieces, offset, length, total, bst, w, want_fwd=True, want_trans=True):
    hist = bst.shape[1]
    rows = length * len(pieces)
    kernel = functools.partial(
        tile_kernel, offset, rows, want_fwd, want_trans, total is not None, [length] * len(pieces)
    )
    args = [*pieces, bst, w]
    if total is not None:
        args.append(total)
    outs = []
    if want_fwd:
        outs += [jax.ShapeDtypeStruct((8, length), F32)] * len(pieces)
    if want_trans:
        outs.append(jax.ShapeDtypeStruct((8, hist), F32))
    out = pl.pallas_call(
        kernel,
        out_shape=tuple(outs),
        in_specs=[VMEM] * len(args),
        out_specs=(VMEM,) * len(outs),
        scratch_shapes=[
            pltpu.VMEM((24, rows), F32),
            pltpu.VMEM((16, rows), BF16),
            pltpu.VMEM((8, rows), F32),
            pltpu.VMEM((16, hist), F32),
            pltpu.VMEM((ROWS, DEPTH), BF16),
            pltpu.VMEM((ROWS, DEPTH), BF16),
            pltpu.VMEM((2 * ROWS, hist // 2), BF16),
            pltpu.VMEM((2 * ROWS, hist // 2), BF16),
            pltpu.VMEM((hist // 2, 2 * ROWS), BF16),
            pltpu.VMEM((hist // 2, 2 * ROWS), BF16),
        ],
        compiler_params=PARAMS,
        cost_estimate=pl.CostEstimate(
            flops=(1 + 2 * want_fwd + 2 * want_trans) * 2 * 256 * rows * hist,
            bytes_accessed=4 * 24 * rows + 4 * DEPTH * hist,
            transcendentals=rows * hist,
        ),
        name="covariance_tiles",
    )(*args)
    fwd = list(out[: len(pieces)]) if want_fwd else []
    return fwd, out[-1] if want_trans else total


def exchange(x, axis, distance):
    size = lax.axis_size(axis)
    return lax.ppermute(x, axis, [(k, k ^ distance) for k in range(size)])


def on_device(hist_features, hist_weights, anal_features, anal_weights, lengthscale, amplitude):
    hist = hist_features.shape[1]
    count = anal_features.shape[1]
    narrow = lax.axis_size("narrow")
    wide = lax.axis_size("wide")
    fwd_scale = 1.0 / math.sqrt(hist * wide * narrow)
    trans_scale = 1.0 / math.sqrt(count * narrow)
    bst, w, own = prepare(
        fwd_scale,
        trans_scale,
        hist_features,
        hist_weights,
        anal_features,
        anal_weights,
        lengthscale[None, :],
        amplitude[None, :],
    )
    pieces = [exchange(own, "narrow", k) for k in range(1, narrow)]
    call = functools.partial(tile_call, bst=bst, w=w)
    first = count // 2
    fwd_a, total = call([own], 0, first, None)
    others, total = call(pieces, 0, count, total)
    received = [exchange(fwd, "narrow", k + 1) for k, fwd in enumerate(others)]
    fwd_b, hist_out = call([own], first, count - first, total)
    forward = jnp.concatenate(fwd_a + fwd_b, axis=1)
    for term in received:
        forward = forward + term
    distance = 1
    while distance < wide:
        steps = [k * distance for k in range(1, min(4, wide // distance))]
        arrived = [exchange(forward, "wide", step) for step in steps]
        for term in arrived:
            forward = forward + term
        distance *= 4
    return forward, hist_out


def solution(mesh):
    in_specs = (
        P(None, ("wide", "narrow")),
        P(None, ("wide", "narrow")),
        P(None, "narrow"),
        P(None, "narrow"),
        P(),
        P(),
    )
    out_specs = (P(None, "narrow"), P(None, ("wide", "narrow")))
    return jax.shard_map(
        on_device, mesh=mesh, in_specs=in_specs, out_specs=out_specs, check_vma=False
    )
```

```python
import functools
import math

import jax
import jax.numpy as jnp
from jax import lax
from jax.experimental import pallas as pl
from jax.experimental.pallas import tpu as pltpu
from jax.sharding import PartitionSpec as P

F32 = jnp.float32
BF16 = jnp.bfloat16
DEPTH = 128
ROWS = 256
COLS = 256
FLIP_ROUND = 2
FLIP_HI = 2
AHEAD = 4


def round_bf16(x):
    return x.astype(BF16).astype(F32)


def split3(x):
    first = round_bf16(x)
    rest = x - first
    second = round_bf16(rest)
    return first, second, round_bf16(rest - second)


def scale_features(features, lengthscale):
    return features / lengthscale * math.sqrt(math.log2(math.e))


def norm_rows(scaled, own_first):
    norms = jnp.sum(scaled * scaled, axis=0, keepdims=True) * -0.5
    parts = split3(norms)
    row = lax.broadcasted_iota(jnp.int32, (16, scaled.shape[1]), 0)
    base = 0 if own_first else 3
    out = jnp.where(row < 6, 1.0, 0.0).astype(F32)
    for k, part in enumerate(parts):
        out = jnp.where(row == base + k, part, out)
    return out


def stack_anal(scaled):
    p1, p2, p3 = split3(scaled)
    zero = jnp.zeros((16, scaled.shape[1]), F32)
    return [p1, p1, p2, p2, p1, p3, norm_rows(scaled, True), zero]


def stack_hist(scaled):
    p1, p2, p3 = split3(scaled)
    zero = jnp.zeros((16, scaled.shape[1]), F32)
    return [p1, p2, p1, p2, p3, p1, norm_rows(scaled, False), zero]


def hi_lo(x):
    hi = x.astype(BF16)
    return hi, (x - hi.astype(F32)).astype(BF16)


def dot(left, right):
    return jnp.dot(left, right, preferred_element_type=F32)


def dot_nt(left, right):
    dims = (((1,), (1,)), ((), ()))
    return lax.dot_general(left, right, dims, preferred_element_type=F32)


def column(row):
    size = row.shape[1]
    at = lax.broadcasted_iota(jnp.int32, (size, size), 0)
    to = lax.broadcasted_iota(jnp.int32, (size, size), 1)
    return jnp.sum(jnp.where(at == to, row, 0.0), axis=1, keepdims=True)


def prep_kernel(fwd_scale, trans_scale, *refs):
    sources, (bst_ref, w_ref, own_ref) = refs[:6], refs[6:9]
    held, sems = refs[9:15], refs[15]
    copies = [
        pltpu.make_async_copy(source, target, sems.at[k])
        for k, (source, target) in enumerate(zip(sources, held))
    ]
    for copy in copies:
        copy.start()
    for copy in copies:
        copy.wait()
    hf_ref, hw_ref, af_ref, aw_ref, ls_ref, amp_ref = held
    hist = hf_ref.shape[1]
    lengthscale = column(ls_ref[...])
    amplitude = column(amp_ref[...])
    own_ref[0:16, :] = scale_features(af_ref[...], lengthscale)
    own_ref[16:24, :] = aw_ref[...] * (amplitude * trans_scale)
    for start in range(0, hist, COLS):
        cols = slice(start, start + COLS)
        stack = stack_hist(scale_features(hf_ref[:, cols], lengthscale))
        for k, rows in enumerate(stack):
            bst_ref[k * 16 : (k + 1) * 16, cols] = rows.astype(BF16)
        weights = hw_ref[:, cols] * (amplitude * fwd_scale)
        hi = round_bf16(weights)
        w_ref[:, cols] = jnp.concatenate([hi, weights - hi], axis=0).astype(BF16)


def tile_kernel(offset, length, want_fwd, want_trans, has_total, counts, *refs):
    refs = list(refs)
    pieces = [refs.pop(0) for _ in counts]
    bst_ref, w_ref = refs.pop(0), refs.pop(0)
    total_ref = refs.pop(0) if has_total else None
    fwd_refs = [refs.pop(0) for _ in counts] if want_fwd else []
    trans_ref = refs.pop(0) if want_trans else None
    anal_ref, u_ref, fwd_ref, acc_ref = refs[0:4]
    left_refs, tile_refs, flip_refs = refs[4:6], refs[6:8], refs[8:10]
    hist = bst_ref.shape[1]
    half = hist // 2
    blocks = length // ROWS

    for k, piece in enumerate(pieces):
        size = length // len(pieces)
        anal_ref[:, k * size : (k + 1) * size] = piece[:, offset : offset + size]
    if want_trans:
        u_hi, u_lo = hi_lo(anal_ref[16:24, :])
        u_ref[...] = jnp.concatenate([u_hi.astype(F32), u_lo.astype(F32)], axis=0).astype(BF16)
        acc_ref[...] = jnp.zeros_like(acc_ref)

    def rows_of(block):
        return pl.ds(pl.multiple_of(block * ROWS, ROWS), ROWS)

    def prep(block, slot):
        stack = jnp.concatenate(stack_anal(anal_ref[0:16, rows_of(block)]), axis=0)
        left_refs[slot][...] = stack.T.astype(BF16)

    def flips_hi(start):
        return start // COLS % FLIP_ROUND < FLIP_HI

    def produce(slot, part, start):
        at = part * half + start
        exponent = dot(left_refs[slot][...], bst_ref[:, at : at + COLS])
        hi, lo = hi_lo(jnp.exp2(exponent))
        tile_refs[part][0:ROWS, start : start + COLS] = hi
        tile_refs[part][ROWS : 2 * ROWS, start : start + COLS] = lo
        if want_fwd:
            flip_refs[part][start : start + COLS, ROWS : 2 * ROWS] = lo.T
            if flips_hi(start):
                flip_refs[part][start : start + COLS, 0:ROWS] = hi.T

    def consume(part, start, u, fwd):
        tile = tile_refs[part][:, start : start + COLS]
        at = part * half + start
        if want_trans:
            acc_ref[:, at : at + COLS] += dot(u, tile)
        if want_fwd:
            w = w_ref[:, at : at + COLS]
            flip = flip_refs[part][start : start + COLS, :]
            if flips_hi(start):
                both = dot(w, flip)
                fwd += both[:, 0:ROWS] + both[:, ROWS : 2 * ROWS]
            else:
                fwd += dot_nt(w, tile[0:ROWS]) + dot(w, flip[:, ROWS : 2 * ROWS])
        return fwd

    def vectors(block):
        u = u_ref[:, rows_of(block)]
        return jnp.concatenate([u, u], axis=1)

    starts = range(0, half, COLS)
    made = [(0, 1), (1, 0), (1, 1), (0, 0)]
    makes = [(slot, part, start) for slot, part in made for start in starts]
    uses = [(k, part, start) for k in range(2) for part in range(2) for start in starts]

    prep(0, 0)
    for start in starts:
        produce(0, 0, start)

    @pl.loop(0, blocks // 2)
    def _(pair):
        block = pair * 2
        prep(block + 1, 1)
        us = [vectors(block), vectors(block + 1)]
        fwds = [jnp.zeros((16, ROWS), F32)] * 2
        for n in range(len(makes) + AHEAD):
            if n == len(makes) // 2:
                prep(jnp.minimum(block + 2, blocks - 1), 0)
            if n < len(makes):
                produce(*makes[n])
            if n >= AHEAD:
                k, part, start = uses[n - AHEAD]
                fwds[k] = consume(part, start, us[k], fwds[k])
        if want_fwd:
            for k, fwd in enumerate(fwds):
                fwd_ref[:, rows_of(block + k)] = fwd[0:8] + fwd[8:16]

    for k, ref in enumerate(fwd_refs):
        size = length // len(pieces)
        ref[...] = fwd_ref[:, k * size : (k + 1) * size]
    if want_trans:
        total = acc_ref[0:8, :] + acc_ref[8:16, :]
        trans_ref[...] = total + total_ref[...] if has_total else total


VMEM = pl.BlockSpec(memory_space=pltpu.VMEM)
PARAMS = pltpu.CompilerParams(vmem_limit_bytes=40 * 1024 * 1024)


def prepare(fwd_scale, trans_scale, *args):
    hist = args[0].shape[1]
    count = args[2].shape[1]
    return pl.pallas_call(
        functools.partial(prep_kernel, fwd_scale, trans_scale),
        out_shape=(
            jax.ShapeDtypeStruct((DEPTH, hist), BF16),
            jax.ShapeDtypeStruct((16, hist), BF16),
            jax.ShapeDtypeStruct((24, count), F32),
        ),
        in_specs=[pl.BlockSpec(memory_space=pltpu.HBM)] * 6,
        out_specs=(VMEM,) * 3,
        scratch_shapes=[pltpu.VMEM(arg.shape, F32) for arg in args]
        + [pltpu.SemaphoreType.DMA((6,))],
        compiler_params=PARAMS,
        name="prepare",
    )(*[pltpu.with_memory_space_constraint(arg, pltpu.HBM) for arg in args])


def tile_call(pieces, offset, length, total, bst, w, want_fwd=True, want_trans=True):
    hist = bst.shape[1]
    rows = length * len(pieces)
    kernel = functools.partial(
        tile_kernel, offset, rows, want_fwd, want_trans, total is not None, [length] * len(pieces)
    )
    args = [*pieces, bst, w]
    if total is not None:
        args.append(total)
    outs = []
    if want_fwd:
        outs += [jax.ShapeDtypeStruct((8, length), F32)] * len(pieces)
    if want_trans:
        outs.append(jax.ShapeDtypeStruct((8, hist), F32))
    out = pl.pallas_call(
        kernel,
        out_shape=tuple(outs),
        in_specs=[VMEM] * len(args),
        out_specs=(VMEM,) * len(outs),
        scratch_shapes=[
            pltpu.VMEM((24, rows), F32),
            pltpu.VMEM((16, rows), BF16),
            pltpu.VMEM((8, rows), F32),
            pltpu.VMEM((16, hist), F32),
            pltpu.VMEM((ROWS, DEPTH), BF16),
            pltpu.VMEM((ROWS, DEPTH), BF16),
            pltpu.VMEM((2 * ROWS, hist // 2), BF16),
            pltpu.VMEM((2 * ROWS, hist // 2), BF16),
            pltpu.VMEM((hist // 2, 2 * ROWS), BF16),
            pltpu.VMEM((hist // 2, 2 * ROWS), BF16),
        ],
        compiler_params=PARAMS,
        cost_estimate=pl.CostEstimate(
            flops=(1 + 2 * want_fwd + 2 * want_trans) * 2 * 256 * rows * hist,
            bytes_accessed=4 * 24 * rows + 4 * DEPTH * hist,
            transcendentals=rows * hist,
        ),
        name="covariance_tiles",
    )(*args)
    fwd = list(out[: len(pieces)]) if want_fwd else []
    return fwd, out[-1] if want_trans else total


def exchange(x, axis, distance):
    size = lax.axis_size(axis)
    return lax.ppermute(x, axis, [(k, k ^ distance) for k in range(size)])


def on_device(hist_features, hist_weights, anal_features, anal_weights, lengthscale, amplitude):
    hist = hist_features.shape[1]
    count = anal_features.shape[1]
    narrow = lax.axis_size("narrow")
    wide = lax.axis_size("wide")
    fwd_scale = 1.0 / math.sqrt(hist * wide * narrow)
    trans_scale = 1.0 / math.sqrt(count * narrow)
    bst, w, own = prepare(
        fwd_scale,
        trans_scale,
        hist_features,
        hist_weights,
        anal_features,
        anal_weights,
        lengthscale[None, :],
        amplitude[None, :],
    )
    pieces = [exchange(own, "narrow", k) for k in range(1, narrow)]
    call = functools.partial(tile_call, bst=bst, w=w)
    first = count // 4 * 3
    fwd_a, total = call([own], 0, first, None)
    others, total = call(pieces, 0, count, total)
    received = [exchange(fwd, "narrow", k + 1) for k, fwd in enumerate(others)]
    fwd_b, hist_out = call([own], first, count - first, total)
    forward = jnp.concatenate(fwd_a + fwd_b, axis=1)
    for term in received:
        forward = forward + term
    distance = 1
    while distance < wide:
        steps = [k * distance for k in range(1, min(4, wide // distance))]
        arrived = [exchange(forward, "wide", step) for step in steps]
        for term in arrived:
            forward = forward + term
        distance *= 4
    return forward, hist_out


def solution(mesh):
    in_specs = (
        P(None, ("wide", "narrow")),
        P(None, ("wide", "narrow")),
        P(None, "narrow"),
        P(None, "narrow"),
        P(),
        P(),
    )
    out_specs = (P(None, "narrow"), P(None, ("wide", "narrow")))
    return jax.shard_map(
        on_device, mesh=mesh, in_specs=in_specs, out_specs=out_specs, check_vma=False
    )
```

```python
import functools
import math

import jax
import jax.numpy as jnp
from jax import lax
from jax.experimental import pallas as pl
from jax.experimental.pallas import tpu as pltpu
from jax.sharding import PartitionSpec as P

F32 = jnp.float32
BF16 = jnp.bfloat16
DEPTH = 128
ROWS = 256
COLS = 256
FLIP_ROUND = 2
FLIP_HI = 2
AHEAD = 4


def round_bf16(x):
    return x.astype(BF16).astype(F32)


def split3(x):
    first = round_bf16(x)
    rest = x - first
    second = round_bf16(rest)
    return first, second, round_bf16(rest - second)


def scale_features(features, lengthscale):
    return features / lengthscale * math.sqrt(math.log2(math.e))


def norm_rows(scaled, own_first):
    norms = jnp.sum(scaled * scaled, axis=0, keepdims=True) * -0.5
    parts = split3(norms)
    row = lax.broadcasted_iota(jnp.int32, (16, scaled.shape[1]), 0)
    base = 0 if own_first else 3
    out = jnp.where(row < 6, 1.0, 0.0).astype(F32)
    for k, part in enumerate(parts):
        out = jnp.where(row == base + k, part, out)
    return out


def stack_anal(scaled):
    p1, p2, p3 = split3(scaled)
    zero = jnp.zeros((16, scaled.shape[1]), F32)
    return [p1, p1, p2, p2, p1, p3, norm_rows(scaled, True), zero]


def stack_hist(scaled):
    p1, p2, p3 = split3(scaled)
    zero = jnp.zeros((16, scaled.shape[1]), F32)
    return [p1, p2, p1, p2, p3, p1, norm_rows(scaled, False), zero]


def hi_lo(x):
    hi = x.astype(BF16)
    return hi, (x - hi.astype(F32)).astype(BF16)


def dot(left, right):
    return jnp.dot(left, right, preferred_element_type=F32)


def dot_nt(left, right):
    dims = (((1,), (1,)), ((), ()))
    return lax.dot_general(left, right, dims, preferred_element_type=F32)


def column(row):
    size = row.shape[1]
    at = lax.broadcasted_iota(jnp.int32, (size, size), 0)
    to = lax.broadcasted_iota(jnp.int32, (size, size), 1)
    return jnp.sum(jnp.where(at == to, row, 0.0), axis=1, keepdims=True)


def prep_kernel(fwd_scale, trans_scale, *refs):
    sources, (bst_ref, w_ref, own_ref) = refs[:6], refs[6:9]
    held, sems = refs[9:15], refs[15]
    copies = [
        pltpu.make_async_copy(source, target, sems.at[k])
        for k, (source, target) in enumerate(zip(sources, held))
    ]
    for copy in copies:
        copy.start()
    for copy in copies:
        copy.wait()
    hf_ref, hw_ref, af_ref, aw_ref, ls_ref, amp_ref = held
    hist = hf_ref.shape[1]
    lengthscale = column(ls_ref[...])
    amplitude = column(amp_ref[...])
    own_ref[0:16, :] = scale_features(af_ref[...], lengthscale)
    own_ref[16:24, :] = aw_ref[...] * (amplitude * trans_scale)
    for start in range(0, hist, COLS):
        cols = slice(start, start + COLS)
        stack = stack_hist(scale_features(hf_ref[:, cols], lengthscale))
        for k, rows in enumerate(stack):
            bst_ref[k * 16 : (k + 1) * 16, cols] = rows.astype(BF16)
        weights = hw_ref[:, cols] * (amplitude * fwd_scale)
        hi = round_bf16(weights)
        w_ref[:, cols] = jnp.concatenate([hi, weights - hi], axis=0).astype(BF16)


def tile_kernel(offset, length, want_fwd, want_trans, has_total, counts, *refs):
    refs = list(refs)
    pieces = [refs.pop(0) for _ in counts]
    bst_ref, w_ref = refs.pop(0), refs.pop(0)
    total_ref = refs.pop(0) if has_total else None
    fwd_refs = [refs.pop(0) for _ in counts] if want_fwd else []
    trans_ref = refs.pop(0) if want_trans else None
    anal_ref, u_ref, fwd_ref, acc_ref = refs[0:4]
    left_refs, tile_refs, flip_refs = refs[4:6], refs[6:8], refs[8:10]
    hist = bst_ref.shape[1]
    half = hist // 2
    blocks = length // ROWS

    for k, piece in enumerate(pieces):
        size = length // len(pieces)
        anal_ref[:, k * size : (k + 1) * size] = piece[:, offset : offset + size]
    if want_trans:
        u_hi, u_lo = hi_lo(anal_ref[16:24, :])
        u_ref[...] = jnp.concatenate([u_hi.astype(F32), u_lo.astype(F32)], axis=0).astype(BF16)
        acc_ref[...] = jnp.zeros_like(acc_ref)

    def rows_of(block):
        return pl.ds(pl.multiple_of(block * ROWS, ROWS), ROWS)

    def prep(block, slot):
        stack = jnp.concatenate(stack_anal(anal_ref[0:16, rows_of(block)]), axis=0)
        left_refs[slot][...] = stack.T.astype(BF16)

    def flips_hi(start):
        return start // COLS % FLIP_ROUND < FLIP_HI

    def produce(slot, part, start):
        at = part * half + start
        exponent = dot(left_refs[slot][...], bst_ref[:, at : at + COLS])
        hi, lo = hi_lo(jnp.exp2(exponent))
        tile_refs[part][0:ROWS, start : start + COLS] = hi
        tile_refs[part][ROWS : 2 * ROWS, start : start + COLS] = lo
        if want_fwd:
            flip_refs[part][start : start + COLS, ROWS : 2 * ROWS] = lo.T
            if flips_hi(start):
                flip_refs[part][start : start + COLS, 0:ROWS] = hi.T

    def consume(part, start, u, fwd):
        tile = tile_refs[part][:, start : start + COLS]
        at = part * half + start
        if want_trans:
            acc_ref[:, at : at + COLS] += dot(u, tile)
        if want_fwd:
            w = w_ref[:, at : at + COLS]
            flip = flip_refs[part][start : start + COLS, :]
            if flips_hi(start):
                both = dot(w, flip)
                fwd += both[:, 0:ROWS] + both[:, ROWS : 2 * ROWS]
            else:
                fwd += dot_nt(w, tile[0:ROWS]) + dot(w, flip[:, ROWS : 2 * ROWS])
        return fwd

    def vectors(block):
        u = u_ref[:, rows_of(block)]
        return jnp.concatenate([u, u], axis=1)

    starts = range(0, half, COLS)
    ahead = min(AHEAD, len(starts) - 1)
    turn = 4 if blocks % 4 == 0 else 2
    made = [(slot % 2, part) for k in range(turn) for slot, part in ((k, 1), (k + 1, 0))]
    makes = [(slot, part, start) for slot, part in made for start in starts]
    uses = [(k, part, start) for k in range(turn) for part in range(2) for start in starts]

    prep(0, 0)
    for start in starts:
        produce(0, 0, start)

    @pl.loop(0, blocks // turn)
    def _(index):
        block = index * turn
        us = [vectors(block + k) for k in range(turn)]
        fwds = [jnp.zeros((16, ROWS), F32)] * turn
        for n in range(len(makes) + ahead):
            k, rest = divmod(n, 2 * len(starts))
            if rest == 0 and k < turn:
                prep(jnp.minimum(block + k + 1, blocks - 1), (k + 1) % 2)
            if n < len(makes):
                produce(*makes[n])
            if n >= ahead:
                k, part, start = uses[n - ahead]
                fwds[k] = consume(part, start, us[k], fwds[k])
        if want_fwd:
            for k, fwd in enumerate(fwds):
                fwd_ref[:, rows_of(block + k)] = fwd[0:8] + fwd[8:16]

    for k, ref in enumerate(fwd_refs):
        size = length // len(pieces)
        ref[...] = fwd_ref[:, k * size : (k + 1) * size]
    if want_trans:
        total = acc_ref[0:8, :] + acc_ref[8:16, :]
        trans_ref[...] = total + total_ref[...] if has_total else total


VMEM = pl.BlockSpec(memory_space=pltpu.VMEM)
PARAMS = pltpu.CompilerParams(vmem_limit_bytes=40 * 1024 * 1024)


def prepare(fwd_scale, trans_scale, *args):
    hist = args[0].shape[1]
    count = args[2].shape[1]
    return pl.pallas_call(
        functools.partial(prep_kernel, fwd_scale, trans_scale),
        out_shape=(
            jax.ShapeDtypeStruct((DEPTH, hist), BF16),
            jax.ShapeDtypeStruct((16, hist), BF16),
            jax.ShapeDtypeStruct((24, count), F32),
        ),
        in_specs=[pl.BlockSpec(memory_space=pltpu.HBM)] * 6,
        out_specs=(VMEM,) * 3,
        scratch_shapes=[pltpu.VMEM(arg.shape, F32) for arg in args]
        + [pltpu.SemaphoreType.DMA((6,))],
        compiler_params=PARAMS,
        name="prepare",
    )(*[pltpu.with_memory_space_constraint(arg, pltpu.HBM) for arg in args])


def tile_call(pieces, offset, length, total, bst, w, want_fwd=True, want_trans=True):
    hist = bst.shape[1]
    rows = length * len(pieces)
    kernel = functools.partial(
        tile_kernel, offset, rows, want_fwd, want_trans, total is not None, [length] * len(pieces)
    )
    args = [*pieces, bst, w]
    if total is not None:
        args.append(total)
    outs = []
    if want_fwd:
        outs += [jax.ShapeDtypeStruct((8, length), F32)] * len(pieces)
    if want_trans:
        outs.append(jax.ShapeDtypeStruct((8, hist), F32))
    out = pl.pallas_call(
        kernel,
        out_shape=tuple(outs),
        in_specs=[VMEM] * len(args),
        out_specs=(VMEM,) * len(outs),
        scratch_shapes=[
            pltpu.VMEM((24, rows), F32),
            pltpu.VMEM((16, rows), BF16),
            pltpu.VMEM((8, rows), F32),
            pltpu.VMEM((16, hist), F32),
            pltpu.VMEM((ROWS, DEPTH), BF16),
            pltpu.VMEM((ROWS, DEPTH), BF16),
            pltpu.VMEM((2 * ROWS, hist // 2), BF16),
            pltpu.VMEM((2 * ROWS, hist // 2), BF16),
            pltpu.VMEM((hist // 2, 2 * ROWS), BF16),
            pltpu.VMEM((hist // 2, 2 * ROWS), BF16),
        ],
        compiler_params=PARAMS,
        cost_estimate=pl.CostEstimate(
            flops=(1 + 2 * want_fwd + 2 * want_trans) * 2 * 256 * rows * hist,
            bytes_accessed=4 * 24 * rows + 4 * DEPTH * hist,
            transcendentals=rows * hist,
        ),
        name="covariance_tiles",
    )(*args)
    fwd = list(out[: len(pieces)]) if want_fwd else []
    return fwd, out[-1] if want_trans else total


def exchange(x, axis, distance):
    size = lax.axis_size(axis)
    return lax.ppermute(x, axis, [(k, k ^ distance) for k in range(size)])


def on_device(hist_features, hist_weights, anal_features, anal_weights, lengthscale, amplitude):
    hist = hist_features.shape[1]
    count = anal_features.shape[1]
    narrow = lax.axis_size("narrow")
    wide = lax.axis_size("wide")
    fwd_scale = 1.0 / math.sqrt(hist * wide * narrow)
    trans_scale = 1.0 / math.sqrt(count * narrow)
    bst, w, own = prepare(
        fwd_scale,
        trans_scale,
        hist_features,
        hist_weights,
        anal_features,
        anal_weights,
        lengthscale[None, :],
        amplitude[None, :],
    )
    pieces = [exchange(own, "narrow", k) for k in range(1, narrow)]
    call = functools.partial(tile_call, bst=bst, w=w)
    first = count // 4 * 3
    fwd_a, total = call([own], 0, first, None)
    others, total = call(pieces, 0, count, total)
    received = [exchange(fwd, "narrow", k + 1) for k, fwd in enumerate(others)]
    fwd_b, hist_out = call([own], first, count - first, total)
    forward = jnp.concatenate(fwd_a + fwd_b, axis=1)
    for term in received:
        forward = forward + term
    distance = 1
    while distance < wide:
        steps = [k * distance for k in range(1, min(4, wide // distance))]
        arrived = [exchange(forward, "wide", step) for step in steps]
        for term in arrived:
            forward = forward + term
        distance *= 4
    return forward, hist_out


def solution(mesh):
    in_specs = (
        P(None, ("wide", "narrow")),
        P(None, ("wide", "narrow")),
        P(None, "narrow"),
        P(None, "narrow"),
        P(),
        P(),
    )
    out_specs = (P(None, "narrow"), P(None, ("wide", "narrow")))
    return jax.shard_map(
        on_device, mesh=mesh, in_specs=in_specs, out_specs=out_specs, check_vma=False
    )
```

```python
import functools
import math

import jax
import jax.numpy as jnp
from jax import lax
from jax.experimental import pallas as pl
from jax.experimental.pallas import tpu as pltpu
from jax.sharding import PartitionSpec as P

F32 = jnp.float32
BF16 = jnp.bfloat16
DEPTH = 128
ROWS = 256
COLS = 256
FLIP_ROUND = 4
FLIP_HI = 3
AHEAD = 4


def round_bf16(x):
    return x.astype(BF16).astype(F32)


def split3(x):
    first = round_bf16(x)
    rest = x - first
    second = round_bf16(rest)
    return first, second, round_bf16(rest - second)


def scale_features(features, lengthscale):
    return features / lengthscale * math.sqrt(math.log2(math.e))


def norm_rows(scaled, own_first):
    norms = jnp.sum(scaled * scaled, axis=0, keepdims=True) * -0.5
    parts = split3(norms)
    row = lax.broadcasted_iota(jnp.int32, (16, scaled.shape[1]), 0)
    base = 0 if own_first else 3
    out = jnp.where(row < 6, 1.0, 0.0).astype(F32)
    for k, part in enumerate(parts):
        out = jnp.where(row == base + k, part, out)
    return out


def stack_anal(scaled):
    p1, p2, p3 = split3(scaled)
    zero = jnp.zeros((16, scaled.shape[1]), F32)
    return [p1, p1, p2, p2, p1, p3, norm_rows(scaled, True), zero]


def stack_hist(scaled):
    p1, p2, p3 = split3(scaled)
    zero = jnp.zeros((16, scaled.shape[1]), F32)
    return [p1, p2, p1, p2, p3, p1, norm_rows(scaled, False), zero]


def hi_lo(x):
    hi = x.astype(BF16)
    return hi, (x - hi.astype(F32)).astype(BF16)


def dot(left, right):
    return jnp.dot(left, right, preferred_element_type=F32)


def dot_nt(left, right):
    dims = (((1,), (1,)), ((), ()))
    return lax.dot_general(left, right, dims, preferred_element_type=F32)


def column(row):
    size = row.shape[1]
    at = lax.broadcasted_iota(jnp.int32, (size, size), 0)
    to = lax.broadcasted_iota(jnp.int32, (size, size), 1)
    return jnp.sum(jnp.where(at == to, row, 0.0), axis=1, keepdims=True)


def prep_kernel(fwd_scale, trans_scale, *refs):
    sources, (bst_ref, w_ref, own_ref) = refs[:6], refs[6:9]
    held, sems = refs[9:15], refs[15]
    copies = [
        pltpu.make_async_copy(source, target, sems.at[k])
        for k, (source, target) in enumerate(zip(sources, held))
    ]
    for copy in copies:
        copy.start()
    for copy in copies:
        copy.wait()
    hf_ref, hw_ref, af_ref, aw_ref, ls_ref, amp_ref = held
    hist = hf_ref.shape[1]
    lengthscale = column(ls_ref[...])
    amplitude = column(amp_ref[...])
    own_ref[0:16, :] = scale_features(af_ref[...], lengthscale)
    own_ref[16:24, :] = aw_ref[...] * (amplitude * trans_scale)
    for start in range(0, hist, COLS):
        cols = slice(start, start + COLS)
        stack = stack_hist(scale_features(hf_ref[:, cols], lengthscale))
        for k, rows in enumerate(stack):
            bst_ref[k * 16 : (k + 1) * 16, cols] = rows.astype(BF16)
        weights = hw_ref[:, cols] * (amplitude * fwd_scale)
        hi = round_bf16(weights)
        w_ref[:, cols] = jnp.concatenate([hi, weights - hi], axis=0).astype(BF16)


def tile_kernel(offset, length, want_fwd, want_trans, has_total, counts, *refs):
    refs = list(refs)
    pieces = [refs.pop(0) for _ in counts]
    bst_ref, w_ref = refs.pop(0), refs.pop(0)
    total_ref = refs.pop(0) if has_total else None
    fwd_refs = [refs.pop(0) for _ in counts] if want_fwd else []
    trans_ref = refs.pop(0) if want_trans else None
    anal_ref, u_ref, fwd_ref, acc_ref = refs[0:4]
    left_refs, tile_refs, flip_refs = refs[4:6], refs[6:8], refs[8:10]
    hist = bst_ref.shape[1]
    half = hist // 2
    blocks = length // ROWS

    for k, piece in enumerate(pieces):
        size = length // len(pieces)
        anal_ref[:, k * size : (k + 1) * size] = piece[:, offset : offset + size]
    if want_trans:
        u_hi, u_lo = hi_lo(anal_ref[16:24, :])
        u_ref[...] = jnp.concatenate([u_hi.astype(F32), u_lo.astype(F32)], axis=0).astype(BF16)
        acc_ref[...] = jnp.zeros_like(acc_ref)

    def rows_of(block):
        return pl.ds(pl.multiple_of(block * ROWS, ROWS), ROWS)

    def prep(block, slot):
        stack = jnp.concatenate(stack_anal(anal_ref[0:16, rows_of(block)]), axis=0)
        left_refs[slot][...] = stack.T.astype(BF16)

    def flips_hi(start):
        return start // COLS % FLIP_ROUND < FLIP_HI

    def produce(slot, part, start):
        at = part * half + start
        exponent = dot(left_refs[slot][...], bst_ref[:, at : at + COLS])
        hi, lo = hi_lo(jnp.exp2(exponent))
        tile_refs[part][0:ROWS, start : start + COLS] = hi
        tile_refs[part][ROWS : 2 * ROWS, start : start + COLS] = lo
        if want_fwd:
            flip_refs[part][start : start + COLS, ROWS : 2 * ROWS] = lo.T
            if flips_hi(start):
                flip_refs[part][start : start + COLS, 0:ROWS] = hi.T

    def consume(part, start, u, fwd):
        tile = tile_refs[part][:, start : start + COLS]
        at = part * half + start
        if want_trans:
            acc_ref[:, at : at + COLS] += dot(u, tile)
        if want_fwd:
            w = w_ref[:, at : at + COLS]
            flip = flip_refs[part][start : start + COLS, :]
            if flips_hi(start):
                both = dot(w, flip)
                fwd += both[:, 0:ROWS] + both[:, ROWS : 2 * ROWS]
            else:
                fwd += dot_nt(w, tile[0:ROWS]) + dot(w, flip[:, ROWS : 2 * ROWS])
        return fwd

    def vectors(block):
        u = u_ref[:, rows_of(block)]
        return jnp.concatenate([u, u], axis=1)

    starts = range(0, half, COLS)
    ahead = min(AHEAD, len(starts) - 1)
    turn = 4 if blocks % 4 == 0 else 2
    made = [(slot % 2, part) for k in range(turn) for slot, part in ((k, 1), (k + 1, 0))]
    makes = [(slot, part, start) for slot, part in made for start in starts]
    uses = [(k, part, start) for k in range(turn) for part in range(2) for start in starts]

    prep(0, 0)
    for start in starts:
        produce(0, 0, start)

    @pl.loop(0, blocks // turn)
    def _(index):
        block = index * turn
        us = [vectors(block + k) for k in range(turn)]
        fwds = [jnp.zeros((16, ROWS), F32)] * turn
        for n in range(len(makes) + ahead):
            k, rest = divmod(n, 2 * len(starts))
            if rest == 0 and k < turn:
                prep(jnp.minimum(block + k + 1, blocks - 1), (k + 1) % 2)
            if n < len(makes):
                produce(*makes[n])
            if n >= ahead:
                k, part, start = uses[n - ahead]
                fwds[k] = consume(part, start, us[k], fwds[k])
        if want_fwd:
            for k, fwd in enumerate(fwds):
                fwd_ref[:, rows_of(block + k)] = fwd[0:8] + fwd[8:16]

    for k, ref in enumerate(fwd_refs):
        size = length // len(pieces)
        ref[...] = fwd_ref[:, k * size : (k + 1) * size]
    if want_trans:
        total = acc_ref[0:8, :] + acc_ref[8:16, :]
        trans_ref[...] = total + total_ref[...] if has_total else total


VMEM = pl.BlockSpec(memory_space=pltpu.VMEM)
PARAMS = pltpu.CompilerParams(vmem_limit_bytes=40 * 1024 * 1024)


def prepare(fwd_scale, trans_scale, *args):
    hist = args[0].shape[1]
    count = args[2].shape[1]
    return pl.pallas_call(
        functools.partial(prep_kernel, fwd_scale, trans_scale),
        out_shape=(
            jax.ShapeDtypeStruct((DEPTH, hist), BF16),
            jax.ShapeDtypeStruct((16, hist), BF16),
            jax.ShapeDtypeStruct((24, count), F32),
        ),
        in_specs=[pl.BlockSpec(memory_space=pltpu.HBM)] * 6,
        out_specs=(VMEM,) * 3,
        scratch_shapes=[pltpu.VMEM(arg.shape, F32) for arg in args]
        + [pltpu.SemaphoreType.DMA((6,))],
        compiler_params=PARAMS,
        name="prepare",
    )(*[pltpu.with_memory_space_constraint(arg, pltpu.HBM) for arg in args])


def tile_call(pieces, offset, length, total, bst, w, want_fwd=True, want_trans=True):
    hist = bst.shape[1]
    rows = length * len(pieces)
    kernel = functools.partial(
        tile_kernel, offset, rows, want_fwd, want_trans, total is not None, [length] * len(pieces)
    )
    args = [*pieces, bst, w]
    if total is not None:
        args.append(total)
    outs = []
    if want_fwd:
        outs += [jax.ShapeDtypeStruct((8, length), F32)] * len(pieces)
    if want_trans:
        outs.append(jax.ShapeDtypeStruct((8, hist), F32))
    out = pl.pallas_call(
        kernel,
        out_shape=tuple(outs),
        in_specs=[VMEM] * len(args),
        out_specs=(VMEM,) * len(outs),
        scratch_shapes=[
            pltpu.VMEM((24, rows), F32),
            pltpu.VMEM((16, rows), BF16),
            pltpu.VMEM((8, rows), F32),
            pltpu.VMEM((16, hist), F32),
            pltpu.VMEM((ROWS, DEPTH), BF16),
            pltpu.VMEM((ROWS, DEPTH), BF16),
            pltpu.VMEM((2 * ROWS, hist // 2), BF16),
            pltpu.VMEM((2 * ROWS, hist // 2), BF16),
            pltpu.VMEM((hist // 2, 2 * ROWS), BF16),
            pltpu.VMEM((hist // 2, 2 * ROWS), BF16),
        ],
        compiler_params=PARAMS,
        cost_estimate=pl.CostEstimate(
            flops=(1 + 2 * want_fwd + 2 * want_trans) * 2 * 256 * rows * hist,
            bytes_accessed=4 * 24 * rows + 4 * DEPTH * hist,
            transcendentals=rows * hist,
        ),
        name="covariance_tiles",
    )(*args)
    fwd = list(out[: len(pieces)]) if want_fwd else []
    return fwd, out[-1] if want_trans else total


def exchange(x, axis, distance):
    size = lax.axis_size(axis)
    return lax.ppermute(x, axis, [(k, k ^ distance) for k in range(size)])


def on_device(hist_features, hist_weights, anal_features, anal_weights, lengthscale, amplitude):
    hist = hist_features.shape[1]
    count = anal_features.shape[1]
    narrow = lax.axis_size("narrow")
    wide = lax.axis_size("wide")
    fwd_scale = 1.0 / math.sqrt(hist * wide * narrow)
    trans_scale = 1.0 / math.sqrt(count * narrow)
    bst, w, own = prepare(
        fwd_scale,
        trans_scale,
        hist_features,
        hist_weights,
        anal_features,
        anal_weights,
        lengthscale[None, :],
        amplitude[None, :],
    )
    pieces = [exchange(own, "narrow", k) for k in range(1, narrow)]
    call = functools.partial(tile_call, bst=bst, w=w)
    first = count // 4 * 3
    fwd_a, total = call([own], 0, first, None)
    others, total = call(pieces, 0, count, total)
    received = [exchange(fwd, "narrow", k + 1) for k, fwd in enumerate(others)]
    fwd_b, hist_out = call([own], first, count - first, total)
    forward = jnp.concatenate(fwd_a + fwd_b, axis=1)
    for term in received:
        forward = forward + term
    distance = 1
    while distance < wide:
        steps = [k * distance for k in range(1, min(4, wide // distance))]
        arrived = [exchange(forward, "wide", step) for step in steps]
        for term in arrived:
            forward = forward + term
        distance *= 4
    return forward, hist_out


def solution(mesh):
    in_specs = (
        P(None, ("wide", "narrow")),
        P(None, ("wide", "narrow")),
        P(None, "narrow"),
        P(None, "narrow"),
        P(),
        P(),
    )
    out_specs = (P(None, "narrow"), P(None, ("wide", "narrow")))
    return jax.shard_map(
        on_device, mesh=mesh, in_specs=in_specs, out_specs=out_specs, check_vma=False
    )
```
